512 devices in a mesh: dp: 8 (over z), seq: 64 (over y, x, core).
Axes of the slice: x: 4, y: 8, z: 8, core: 2. Of those that a mesh axis runs over, the one named last changes fastest.
Arguments:
- frames_in: bfloat16 [8, 256, 2, 16, 32, 384], P('dp', 'seq'), may hold values from -6 to 6
- clip_frames: int32 [8, 32], P('dp'), may hold values from 1 to 21, 256 in all within a row
- res_ids: int32 [8, 32], P('dp'), may hold values from 0 to 1
- token_dest: int32 [8, 32768, 1], P('dp', 'seq'), may hold values from 0 to 511; in each aligned block of 512 rows (0 to 511, 512 to 1023, ..., all dimensions but the last counted through in order) at most 2 rows name the same one
- tconv_weight: bfloat16 [3, 384, 384], replicated, may hold values from -0.1875 to 0.1875
- tconv_bias: float32 [384], replicated, may hold values from -3 to 3
- head_gain: float32 [384], replicated, may hold values from 0.1 to 1.9
- head_weight: bfloat16 [3, 3, 3, 384, 16], replicated, may hold values from -0.0625 to 0.0625
- head_bias: float32 [16], replicated, may hold values from -3 to 3
- latent_mean: float32 [16], replicated, may hold values from -0.5 to 0.5
- latent_scale: float32 [16], replicated, may hold values from 0.5 to 2
Outputs:
- latent_slots: bfloat16 [8, 64, 512, 128], P('dp', 'seq')
The draws below stay inside these ranges and needn't reach their ends.
Inputs may be any that keep to these rules, and one draw needn't show every extreme that they name: `clip_frames`: the 32 clips of a row fill its 256 latent frames exactly; some clip of each row has 21. `res_ids`: 0 marks a 480p clip, 1 a 720p clip. `token_dest`: among the 512 patches of one device no destination appears more than 2 times, a bound that some block reaches.
All inputs are finite; a program needn't handle non-finite values.
Results may differ from the reference program's by a relative error of at most 0.0055.
Values may be sent and summed in bfloat16 or wider, within the bound.
A program may use at most 64 MiB of HBM per device.

```python
import math
import jax
import jax.numpy as jnp
import numpy as np
from jax import lax

C = 384
ZD = 16
LH = 16
LW = 32
MAXLEN = 21
LFRAMES = 256
CLIPS = 32
TOKD = 512
CAP = 2
N_DP = 8
N_SEQ = 64


def plant(array, own_key, smallest, high):
    shape = array.shape
    place = [jax.random.randint(jax.random.fold_in(own_key, axis), (), 0, shape[axis]) for axis in range(len(shape))]
    array = array.at[tuple(place)].set(smallest)
    longest = shape.index(max(shape))
    place[longest] = (place[longest] + 1) % shape[longest]
    return array.at[tuple(place)].set(high)


def levels(rng, shape, pieces, least, high):
    factor_of, own = 1.0, jax.random.fold_in(rng, 6)
    for axis_at, parts in pieces:
        draws = jnp.exp(jax.random.uniform(jax.random.fold_in(own, axis_at), (parts,), jnp.float32, least / len(pieces), high / len(pieces)))
        factor_of = factor_of * jnp.repeat(draws, shape[axis_at] // parts).reshape([-1 if axis == axis_at else 1 for axis in range(len(shape))])
    return factor_of


def profile(amount, total, most, lean):
    loads = [(1 << 20) // math.isqrt(grade ** lean) + 1 for grade in range(2, amount + 1)]
    surplus, given = total - most - (amount - 1), [1] * (amount - 1)
    while surplus > 0:
        candidates = [i for i in range(amount - 1) if given[i] < most]
        mass, remaining = sum([loads[i] for i in candidates]), surplus
        for i in candidates:
            extra = min(most - given[i], max(1, remaining * loads[i] // mass), surplus)
            given[i] = given[i] + extra
            surplus = surplus - extra
    return np.array([most] + given)


def uneven(rng, count, total, limit, slope):
    if count == 2:
        one = jax.random.randint(rng, (), max(1, total - limit), min(limit, total - 1) + 1)
        return jnp.stack([one, total - one])
    sizes = jnp.asarray(profile(count, total, limit, slope), jnp.int32)
    couples = (count - 1) // 2
    donor, sink = sizes[1:1 + 2 * couples:2], sizes[2:2 + 2 * couples:2]
    slack = jnp.minimum(donor - 1, limit - sink)
    shifted = jax.random.randint(jax.random.fold_in(rng, 1), (couples,), 0, 1 << 20) % (slack + 1)
    sizes = sizes.at[1:1 + 2 * couples:2].set(donor - shifted).at[2:2 + 2 * couples:2].set(sink + shifted)
    return sizes[jax.random.permutation(jax.random.fold_in(rng, 2), count)]


def routed_block(rng, own, number, rows, amount, top, most, slope):
    order = jax.random.permutation(rng, amount)
    packed, common = portions_of(amount, rows * top, most, slope, True), portions_of(amount, rows * top, most, slope, False)
    places = jnp.arange(amount)

    def named(tallies, rotation):
        used = int((tallies > 0).sum())
        fixed = max(1, used // 4)
        shifted = fixed + (places - fixed + rotation * (used - fixed)) % max(1, amount - fixed)
        return jnp.zeros((amount,), jnp.int32).at[order[jnp.where(places < fixed, places, shifted)]].set(jnp.asarray(tallies, jnp.int32))

    tallies = jnp.where(number % 4 == 0, named(packed, number // 4), named(common, number - number // 4 - 1))
    mixed = jax.random.permutation(jax.random.fold_in(own, 3), amount)
    donor, sink = mixed[0:amount // 2 * 2:2], mixed[1:amount // 2 * 2:2]
    room = jnp.minimum(tallies[donor] - 1, most - tallies[sink]) // 2
    room = jnp.where((donor == order[0]) | (sink == order[0]) | (tallies[sink] == 0), 0, jnp.maximum(room, 0))
    shifted = jax.random.randint(jax.random.fold_in(own, 4), (amount // 2,), 0, 1 << 20) % (room + 1)
    tallies = tallies.at[donor].add(-shifted).at[sink].add(shifted)
    items = jnp.searchsorted(jnp.cumsum(tallies), jnp.arange(rows * top), side="right").astype(jnp.int32)
    listing = items.reshape(top, rows).T
    listing = listing[jax.random.permutation(jax.random.fold_in(own, 1), rows)]
    rotation = jax.random.randint(jax.random.fold_in(own, 2), (rows, 1), 0, top)
    return jnp.take_along_axis(listing, (jnp.arange(top)[None, :] + rotation) % top, axis=1)


def portions_of(number_of, total, reach, slope, full):
    weights = [(1 << 20) // math.isqrt(standing ** slope) + 1 for standing in range(1, number_of + 1)]
    largest = reach if full else min(reach, max(-(-total // number_of), total * weights[0] // sum(weights)))
    least = 1 if total - largest >= number_of - 1 else 0
    holding, spare = [largest] + [least] * (number_of - 1), total - largest - least * (number_of - 1)
    while spare > 0:
        candidates = [i for i in range(1, number_of) if holding[i] < largest] or [i for i in range(1, number_of) if holding[i] < reach]
        pool, remaining = sum([weights[i] for i in candidates]), spare
        for i in candidates:
            more = min(reach - holding[i], max(1, remaining * weights[i] // pool), spare)
            holding[i] = holding[i] + more
            spare = spare - more
    return np.array(holding)


def scatter_about(rng, dims, deviation, limit, shards=(), held_as=jnp.bfloat16):
    factor_of = levels(rng, dims, shards, -0.22, 0.18) if shards else 1.0
    result = jax.random.normal(rng, dims, jnp.float32) * deviation * factor_of
    return jnp.minimum(jnp.maximum(result, -limit), limit).astype(held_as)


def setup_inputs(seed: int = 0) -> dict:
    streams_of = jax.random.split(jax.random.key(seed), 12)
    frames_in = scatter_about(streams_of[0], (N_DP, LFRAMES, 2, LH, LW, C), 1.0, 6.0, ((0, 8), (1, 64)))
    clip_frames = jax.vmap(lambda own: uneven(own, CLIPS, LFRAMES, MAXLEN, 2))(jax.random.split(streams_of[1], N_DP)).reshape((N_DP, CLIPS)).astype(jnp.int32)
    res_ids = plant(jax.random.randint(streams_of[2], (N_DP, CLIPS), 0, 2), jax.random.fold_in(streams_of[2], 1), 0, 1).astype(jnp.int32)
    token_dest_keys = jax.random.split(jax.random.fold_in(streams_of[3], 1), N_DP * (N_SEQ * TOKD) // TOKD)
    token_dest_turns = jax.random.permutation(jax.random.fold_in(streams_of[3], 3), N_DP * (N_SEQ * TOKD) // TOKD)
    token_dest = jax.vmap(lambda own, number: routed_block(jax.random.fold_in(streams_of[3], 2), own, number, TOKD, N_DP * N_SEQ, 1, CAP, 2))(token_dest_keys, token_dest_turns).reshape((N_DP, N_SEQ * TOKD, 1))
    tconv_weight = scatter_about(streams_of[4], (3, C, C), (3 * C) ** -0.5, 0.1875)
    tconv_bias = scatter_about(streams_of[5], (C,), 0.5, 3.0, (), jnp.float32)
    head_gain = jnp.clip(1.0 + 0.18 * jax.random.normal(streams_of[6], (C,), jnp.float32), 0.1, 1.9)
    head_weight = scatter_about(streams_of[7], (3, 3, 3, C, ZD), (27 * C) ** -0.5, 0.0625)
    head_bias = scatter_about(streams_of[8], (ZD,), 0.5, 3.0, (), jnp.float32)
    latent_mean = jnp.clip(jax.random.uniform(streams_of[9], (ZD,), jnp.float32, -0.5, 0.5), -0.5, 0.5)
    latent_scale = jnp.clip(jnp.exp(jax.random.uniform(streams_of[10], (ZD,), jnp.float32, math.log(0.5), math.log(2.0))), 0.5, 2.0)
    return {"frames_in": frames_in, "clip_frames": clip_frames, "res_ids": res_ids, "token_dest": token_dest, "tconv_weight": tconv_weight, "tconv_bias": tconv_bias, "head_gain": head_gain, "head_weight": head_weight, "head_bias": head_bias, "latent_mean": latent_mean, "latent_scale": latent_scale}


def clip_lookup(lengths, resolution_ids, frame_index):
    clip_ends = jnp.cumsum(lengths).astype(jnp.int32)
    clip_starts = (clip_ends - lengths).astype(jnp.int32)
    belongs = (frame_index[:, None] >= clip_starts[None, :]) & (frame_index[:, None] < clip_ends[None, :])
    clip_start = lax.optimization_barrier(jnp.sum(jnp.where(belongs, clip_starts[None, :], 0), axis=1)).astype(jnp.int32)
    resolution = lax.optimization_barrier(jnp.sum(jnp.where(belongs, resolution_ids[None, :], 0), axis=1)).astype(jnp.int32)
    return (clip_start, resolution)

def temporal_section(earlier, local_frames, tconv_weight, tconv_bias, first_mask):
    frame_count = local_frames.shape[0]
    height = local_frames.shape[2]
    columns = local_frames.shape[3]
    channels = local_frames.shape[4]
    temporal = jnp.dot(earlier.reshape(-1, channels), tconv_weight[0], preferred_element_type=jnp.float32)
    temporal = temporal + jnp.dot(local_frames[:, 0].reshape(-1, channels), tconv_weight[1], preferred_element_type=jnp.float32)
    temporal = temporal + jnp.dot(local_frames[:, 1].reshape(-1, channels), tconv_weight[2], preferred_element_type=jnp.float32)
    temporal = temporal.reshape(frame_count, height, columns, channels) + tconv_bias
    passed = local_frames[:, 1].astype(jnp.float32)
    return jnp.where(first_mask[:, None, None, None], passed, temporal).astype(jnp.bfloat16)

def activate(section_out, head_gain, picture_limit):
    columns = section_out.shape[2]
    values = section_out.astype(jnp.float32)
    mean_square = lax.optimization_barrier(jnp.mean(values * values, axis=-1, keepdims=True))
    normalized = values * lax.rsqrt(mean_square + 1e-06) * head_gain
    inside = (jnp.arange(columns, dtype=jnp.int32)[None, :] < picture_limit[:, None]).astype(jnp.float32)
    activation = (jax.nn.silu(normalized) * inside[:, None, :, None]).astype(jnp.bfloat16)
    return (activation, inside)

def spatial_taps(products, k, latent_dim):
    height = products.shape[1] - 2
    columns = products.shape[2] - 2
    running = jnp.zeros((products.shape[0], height, columns, latent_dim), jnp.float32)
    for a in range(3):
        for b in range(3):
            column = ((k * 3 + a) * 3 + b) * latent_dim
            running = running + products[:, a:a + height, b:b + columns, column:column + latent_dim]
    return running

def encode_group(frames, lengths, resolution_ids, tconv_weight, tconv_bias, head_gain, head_matrix, head_bias, latent_mean, latent_scale):
    frame_count = frames.shape[0]
    height = frames.shape[2]
    columns = frames.shape[3]
    channels = frames.shape[4]
    latent_dim = head_bias.shape[0]
    frame_index = jnp.arange(frame_count, dtype=jnp.int32)
    clip_start, resolution = clip_lookup(lengths, resolution_ids, frame_index)
    picture_limit = jnp.where(resolution == 1, columns, columns * 13 // 20).astype(jnp.int32)
    earlier = jnp.concatenate([jnp.zeros_like(frames[:1, 1]), frames[:-1, 1]], axis=0)
    section_out = temporal_section(earlier, frames, tconv_weight, tconv_bias, frame_index == clip_start)
    activation, inside = activate(section_out, head_gain, picture_limit)
    padded = jnp.pad(activation, ((2, 0), (1, 1), (1, 1), (0, 0)))
    products = jnp.dot(padded.reshape(-1, channels), head_matrix, preferred_element_type=jnp.float32)
    products = products.reshape(frame_count + 2, height + 2, columns + 2, head_matrix.shape[1])
    head_out = jnp.zeros((frame_count, height, columns, latent_dim), jnp.float32)
    for k in range(3):
        in_clip = (frame_index - 2 + k >= clip_start).astype(jnp.float32)
        head_out = head_out + spatial_taps(products[k:k + frame_count], k, latent_dim) * in_clip[:, None, None, None]
    head_out = head_out + head_bias
    latent = ((head_out - latent_mean) * latent_scale * inside[:, None, :, None]).astype(jnp.bfloat16)
    patches = latent.reshape(frame_count, height // 2, 2, columns // 2, 2, latent_dim)
    return patches.transpose(0, 1, 3, 2, 4, 5).reshape(-1, 4 * latent_dim)

def reference(frames_in, clip_frames, res_ids, token_dest, tconv_weight, tconv_bias, head_gain, head_weight, head_bias, latent_mean, latent_scale):
    head_matrix = jnp.transpose(head_weight, (3, 0, 1, 2, 4)).reshape(C, 27 * ZD)

    def encode_one(clip_group):
        frames, lengths, resolution_ids = clip_group
        return encode_group(frames, lengths, resolution_ids, tconv_weight, tconv_bias, head_gain, head_matrix, head_bias, latent_mean, latent_scale)
    patches = lax.map(encode_one, (frames_in, clip_frames, res_ids))
    destinations = N_DP * N_SEQ
    sources = patches.reshape(destinations, TOKD, 4 * ZD)
    destination = token_dest.reshape(destinations, TOKD).astype(jnp.int32)

    def rank_row(route_row):
        matches = (route_row[:, None] == jnp.arange(destinations, dtype=jnp.int32)[None, :]).astype(jnp.int32)
        before = (jnp.cumsum(matches, axis=0).astype(jnp.int32) - matches) * matches
        return lax.optimization_barrier(jnp.sum(before, axis=1)).astype(jnp.int32)
    ranking = lax.map(rank_row, destination)
    source = jnp.broadcast_to(jnp.arange(destinations, dtype=jnp.int32)[:, None], (destinations, TOKD))
    slots = jnp.zeros((destinations, destinations, CAP, 4 * ZD), jnp.bfloat16)
    slots = slots.at[destination, source, ranking].set(sources)
    return slots.reshape(N_DP, N_SEQ, destinations, CAP * 4 * ZD)
```

```python
import functools

import jax
import jax.numpy as jnp
from jax import lax
from jax.experimental import pallas as pl
from jax.experimental.pallas import tpu as pltpu
from jax.sharding import PartitionSpec as P

CORES = 2


def reorder(rows, source_of):
    target = lax.broadcasted_iota(jnp.int32, (rows, rows), 0)
    source = lax.broadcasted_iota(jnp.int32, (rows, rows), 1)
    return jnp.where(source == source_of(target), 1.0, 0.0).astype(jnp.bfloat16)


def moved(matrix, rows):
    return jnp.dot(matrix, rows, preferred_element_type=jnp.float32).astype(jnp.bfloat16)


def exchange_kernel(replicas, places, rows_ref, out_ref, first, middle, last, send_sem, recv_sem):
    near = replicas * CORES
    total = near * places
    replica = lax.axis_index("dp")
    shard = lax.axis_index("seq")
    place = lax.div(shard, CORES)
    core = lax.rem(shard, CORES)
    mine = replica * CORES + core

    def near_device(step):
        index = lax.rem(mine + step, near)
        return index, (lax.div(index, CORES), place * CORES + lax.rem(index, CORES))

    def far_device(step):
        index = lax.rem(place + step, places)
        return index, (replica, index * CORES + core)

    barrier = pltpu.get_barrier_semaphore()

    def greet(find):
        def body(step, carry):
            pl.semaphore_signal(
                barrier, inc=1, device_id=find(step)[1], device_id_type=pl.DeviceIdType.MESH
            )
            return carry
        return body

    lax.fori_loop(1, near, greet(near_device), 0)
    lax.fori_loop(1, places, greet(far_device), 0)
    pl.semaphore_wait(barrier, near - 1 + places - 1)

    def near_send(step, carry):
        index, device = near_device(step)
        pltpu.make_async_remote_copy(
            src_ref=rows_ref.at[pl.ds(index * places, places)],
            dst_ref=first.at[pl.ds(mine * places, places)],
            send_sem=send_sem.at[0],
            recv_sem=recv_sem.at[0],
            device_id=device,
            device_id_type=pl.DeviceIdType.MESH,
        ).start()
        return carry

    lax.fori_loop(1, near, near_send, 0)
    own = pl.ds(mine * places, places)
    first[own, :] = rows_ref[own, :]
    turn = reorder(total, lambda row: lax.rem(row, near) * places + lax.div(row, near))
    arrived = first.at[pl.ds(0, (near - 1) * places)]
    pltpu.make_async_copy(arrived, arrived, recv_sem.at[0]).wait()
    middle[...] = moved(turn, first[...])

    def far_send(step, carry):
        index, device = far_device(step)
        pltpu.make_async_remote_copy(
            src_ref=middle.at[pl.ds(index * near, near)],
            dst_ref=last.at[pl.ds(place * near, near)],
            send_sem=send_sem.at[1],
            recv_sem=recv_sem.at[1],
            device_id=device,
            device_id_type=pl.DeviceIdType.MESH,
        ).start()
        return carry

    lax.fori_loop(1, places, far_send, 0)
    own = pl.ds(place * near, near)
    last[own, :] = middle[own, :]

    def slot(row):
        source_replica = lax.div(row, places * CORES)
        rest = lax.rem(row, places * CORES)
        return lax.div(rest, CORES) * near + source_replica * CORES + lax.rem(rest, CORES)

    back = reorder(total, slot)
    arrived = last.at[pl.ds(0, (places - 1) * near)]
    pltpu.make_async_copy(arrived, arrived, recv_sem.at[1]).wait()
    out_ref[...] = moved(back, last[...])
    sent = rows_ref.at[pl.ds(0, (near - 1) * places)]
    pltpu.make_async_copy(sent, sent, send_sem.at[0]).wait()
    sent = middle.at[pl.ds(0, (places - 1) * near)]
    pltpu.make_async_copy(sent, sent, send_sem.at[1]).wait()


def exchange(rows, replicas, shards):
    total, width = rows.shape
    places = shards // CORES
    return pl.pallas_call(
        functools.partial(exchange_kernel, replicas, places),
        out_shape=jax.ShapeDtypeStruct((total, width), jnp.bfloat16),
        in_specs=[pl.BlockSpec(memory_space=pltpu.VMEM)],
        out_specs=pl.BlockSpec(memory_space=pltpu.VMEM),
        scratch_shapes=[
            pltpu.VMEM((total, width), jnp.bfloat16),
            pltpu.VMEM((total, width), jnp.bfloat16),
            pltpu.VMEM((total, width), jnp.bfloat16),
            pltpu.SemaphoreType.DMA((2,)),
            pltpu.SemaphoreType.DMA((2,)),
        ],
        compiler_params=pltpu.CompilerParams(collective_id=0, has_side_effects=True),
    )(rows)


def from_behind(value, axis, steps):
    count = lax.axis_size(axis)
    first, last = (max(0, -steps), min(count, count - steps))
    return lax.ppermute(value, axis, [(source, source + steps) for source in range(first, last)])


def clip_lookup(lengths, resolution_ids, frame_index):
    clip_ends = jnp.cumsum(lengths)
    clip_starts = clip_ends - lengths
    belongs = (frame_index[:, None] >= clip_starts[None, :]) & (
        frame_index[:, None] < clip_ends[None, :]
    )
    clip_start = jnp.sum(jnp.where(belongs, clip_starts[None, :], 0), axis=1)
    resolution = jnp.sum(jnp.where(belongs, resolution_ids[None, :], 0), axis=1)
    return (clip_start, resolution)


def temporal_section(earlier, local_frames, tconv_weight, tconv_bias, first_mask):
    frame_count = local_frames.shape[0]
    height = local_frames.shape[2]
    columns = local_frames.shape[3]
    channels = local_frames.shape[4]
    temporal = jnp.dot(
        earlier.reshape(-1, channels), tconv_weight[0], preferred_element_type=jnp.float32
    )
    temporal = temporal + jnp.dot(
        local_frames[:, 0].reshape(-1, channels),
        tconv_weight[1],
        preferred_element_type=jnp.float32,
    )
    temporal = temporal + jnp.dot(
        local_frames[:, 1].reshape(-1, channels),
        tconv_weight[2],
        preferred_element_type=jnp.float32,
    )
    temporal = temporal.reshape(frame_count, height, columns, channels) + tconv_bias
    passed = local_frames[:, 1].astype(jnp.float32)
    return jnp.where(first_mask[:, None, None, None], passed, temporal).astype(jnp.bfloat16)


def activate(section_out, head_gain, picture_limit):
    columns = section_out.shape[2]
    values = section_out.astype(jnp.float32)
    mean_square = jnp.mean(values * values, axis=-1, keepdims=True)
    normalized = values * lax.rsqrt(mean_square + 1e-06) * head_gain
    inside = (jnp.arange(columns, dtype=jnp.int32)[None, :] < picture_limit[:, None]).astype(
        jnp.float32
    )
    activation = (jax.nn.silu(normalized) * inside[:, None, :, None]).astype(jnp.bfloat16)
    return (activation, inside)


def flat_taps(products, k, height, stride):
    span = height * stride
    running = jnp.zeros(products.shape[1:3] + (span,), jnp.float32)
    for a in range(3):
        for b in range(3):
            offset = a * stride + b
            running = running + products[(k * 3 + a) * 3 + b, :, :, offset : offset + span]
    return running


def on_device(
    frames_in,
    clip_frames,
    res_ids,
    token_dest,
    tconv_weight,
    tconv_bias,
    head_gain,
    head_weight,
    head_bias,
    latent_mean,
    latent_scale,
):
    local_frames = frames_in[0]
    frame_count = local_frames.shape[0]
    height = local_frames.shape[2]
    columns = local_frames.shape[3]
    channels = local_frames.shape[4]
    latent_dim = head_weight.shape[-1]
    stride = columns + 2
    first_frame = lax.axis_index("seq") * frame_count
    lengths = clip_frames[0]
    resolution_ids = res_ids[0]
    frame_index = first_frame + jnp.arange(frame_count, dtype=jnp.int32)
    clip_start, resolution = clip_lookup(lengths, resolution_ids, frame_index)
    picture_limit = jnp.where(resolution == 1, columns, columns * 13 // 20).astype(jnp.int32)
    carried = from_behind(local_frames[frame_count - 1, 1], "seq", 1)
    earlier = jnp.concatenate([carried[None], local_frames[: frame_count - 1, 1]], axis=0)
    section_out = temporal_section(
        earlier, local_frames, tconv_weight, tconv_bias, frame_index == clip_start
    )
    activation, inside = activate(section_out, head_gain, picture_limit)
    head_rows = jnp.transpose(head_weight, (0, 1, 2, 4, 3)).reshape(27 * latent_dim, channels)
    head_out = jnp.zeros((latent_dim, frame_count, height * stride), jnp.float32)
    received = from_behind(activation[frame_count - 2 :], "seq", 1)
    frames_act = jnp.concatenate([received, activation], axis=0)
    padded = jnp.pad(frames_act, ((0, 0), (1, 2), (1, 1), (0, 0)))
    products = lax.dot_general(
        head_rows,
        padded.reshape(-1, channels),
        (((1,), (1,)), ((), ())),
        preferred_element_type=jnp.float32,
    )
    products = products.reshape(27, latent_dim, frames_act.shape[0], (height + 3) * stride)
    for k in range(3):
        in_clip = (frame_index - 2 + k >= clip_start).astype(jnp.float32)
        head_out = (
            head_out
            + flat_taps(products[:, :, k : k + frame_count], k, height, stride)
            * in_clip[None, :, None]
        )
    head_out = head_out.reshape(latent_dim, frame_count, height, stride)[:, :, :, :columns]
    head_out = head_out + head_bias[:, None, None, None]
    latent = (
        (head_out - latent_mean[:, None, None, None])
        * latent_scale[:, None, None, None]
        * inside[None, :, None, :]
    ).astype(jnp.bfloat16)
    patches = latent.reshape(latent_dim, frame_count, height // 2, 2, columns // 2, 2)
    features = patches.transpose(3, 5, 0, 1, 2, 4).reshape(4 * latent_dim, -1)
    token_count = features.shape[1]
    replicas = lax.axis_size("dp")
    shards = lax.axis_size("seq")
    destinations = replicas * shards
    capacity = max(2, 2 * token_count // destinations)
    destination = token_dest[0, :, 0]
    matches = (destination[:, None] == jnp.arange(destinations, dtype=jnp.int32)[None, :]).astype(
        jnp.int32
    )
    before = (jnp.cumsum(matches, axis=0) - matches) * matches
    ranking = jnp.sum(before, axis=1)
    places = shards // CORES
    ordered = (
        (destination // shards * CORES + destination % CORES) * places
        + destination % shards // CORES
    )
    slot_index = ordered * capacity + ranking
    placement = (
        slot_index[:, None] == jnp.arange(destinations * capacity, dtype=jnp.int32)[None, :]
    ).astype(jnp.bfloat16)
    buffer = jnp.einsum(
        "ts,ft->sf", placement, features, preferred_element_type=jnp.float32
    ).astype(jnp.bfloat16)
    buffer = buffer.reshape(destinations, capacity * 4 * latent_dim)
    received_slots = exchange(buffer, replicas, shards)
    return received_slots.reshape(1, 1, destinations, capacity * 4 * latent_dim)


def solution(mesh):
    in_specs = (
        P("dp", "seq", None, None, None, None),
        P("dp", None),
        P("dp", None),
        P("dp", "seq", None),
        P(),
        P(),
        P(),
        P(),
        P(),
        P(),
        P(),
    )
    out_specs = P("dp", "seq", None, None)
    return jax.shard_map(
        on_device, mesh=mesh, in_specs=in_specs, out_specs=out_specs, check_vma=False
    )
```

```python
import functools

import jax
import jax.numpy as jnp
from jax import lax
from jax.experimental import pallas as pl
from jax.experimental.pallas import tpu as pltpu
from jax.sharding import PartitionSpec as P

CORES = 2
ALONG_X = 4
CHUNKS = 4
MESH = pl.DeviceIdType.MESH
F32 = jnp.float32
BF16 = jnp.bfloat16


def iota(shape, axis):
    return lax.broadcasted_iota(jnp.int32, shape, axis)


def reorder(rows, source_of):
    source = source_of(iota((rows, 1), 0))
    return jnp.where(iota((rows, rows), 1) == source, 1.0, 0.0).astype(BF16)


def column_of(row):
    count = row.shape[1]
    diagonal = iota((count, count), 0) == iota((count, count), 1)
    return jnp.sum(jnp.where(diagonal, row, 0.0), axis=1, keepdims=True)


def frame_facts(lengths, resolutions, first_frame, total_frames, columns):
    clips = lengths.shape[1]
    earlier = iota((clips, clips), 1) < iota((clips, clips), 0)
    own = iota((clips, clips), 1) == iota((clips, clips), 0)
    starts = jnp.sum(jnp.where(earlier, lengths, 0.0), axis=1, keepdims=True)
    ends = starts + column_of(lengths)
    resolution = jnp.sum(jnp.where(own, resolutions, 0.0), axis=1, keepdims=True)
    frame = (first_frame + iota((clips, 128), 1)).astype(F32)
    belongs = (frame >= starts) & (frame < ends)
    start = jnp.sum(jnp.where(belongs, starts, 0.0), axis=0, keepdims=True)
    kind = jnp.sum(jnp.where(belongs, resolution, 0.0), axis=0, keepdims=True)
    frame = frame[:1]
    exists = frame < float(total_frames)
    first = jnp.where(frame == start, 1.0, 0.0)
    one = jnp.where((frame - 1.0 >= start) & exists, 1.0, 0.0)
    two = jnp.where((frame - 2.0 >= start) & exists, 1.0, 0.0)
    limit = jnp.where(kind == 1.0, float(columns), float(columns * 13 // 20))
    return first, one, two, limit


def pick(row, index):
    return jnp.sum(jnp.where(iota(row.shape, 1) == index, row, 0.0), axis=1, keepdims=True)


def spatial_sum(taps, latent_dim, columns):
    cells = taps.shape[1]
    band = 3 * latent_dim
    cell = iota((1, cells), 1)
    column = lax.rem(cell, columns)
    above = jnp.where(cell >= columns, pltpu.roll(taps[:band], columns, 1), 0.0)
    below = jnp.where(cell < cells - columns, pltpu.roll(taps[2 * band :], cells - columns, 1), 0.0)
    rows = taps[band : 2 * band] + above + below
    left = jnp.where(column >= 1, pltpu.roll(rows[:latent_dim], 1, 1), 0.0)
    right = jnp.where(column < columns - 1, pltpu.roll(rows[2 * latent_dim :], cells - 1, 1), 0.0)
    return rows[latent_dim : 2 * latent_dim] + left + right


def activated(section, passed, first, gain, limit, columns):
    rows, channels = section.shape
    section = jnp.where(first > 0.5, passed.astype(F32), section).astype(BF16).astype(F32)
    mean_square = jnp.sum(section * section, axis=1, keepdims=True) * (1.0 / channels)
    column = lax.rem(iota((rows, 1), 0), columns).astype(F32)
    inside = jnp.where(column < limit, 0.5, 0.0)
    half = section * (lax.rsqrt(mean_square + 1e-06) * 0.5) * gain
    return (half * 2.0 * (inside + inside * jnp.tanh(half))).astype(BF16)


def encode_kernel(
    replicas,
    places,
    height,
    columns,
    frames_hbm,
    clip_hbm,
    res_hbm,
    dest_hbm,
    tconv_hbm,
    bias_hbm,
    gain_hbm,
    head_hbm,
    head_bias_hbm,
    mean_hbm,
    scale_hbm,
    out_ref,
    frames,
    clip,
    res,
    dest,
    tconv,
    bias,
    gain,
    head,
    head_bias,
    mean,
    scale,
    carried,
    halo_in,
    halo_out,
    section,
    active,
    products,
    latents,
    match,
    turn,
    back,
    unpatch,
    outgoing,
    first_stage,
    middle,
    last_stage,
    load_sem,
    carry_send,
    carry_recv,
    halo_sem,
    ready_sem,
    send_sem,
    recv_sem,
):
    near = replicas * CORES
    total = near * places
    shards = places * CORES
    along_y = places // ALONG_X
    frame_count = frames.shape[0] // 2
    cells, channels = frames.shape[1:]
    latent_dim = head_bias.shape[1]
    taps = 9 * latent_dim
    replica = lax.axis_index("dp")
    shard = lax.axis_index("seq")
    place = lax.div(shard, CORES)
    core = lax.rem(shard, CORES)
    x = lax.rem(place, ALONG_X)
    y = lax.div(place, ALONG_X)
    mine = replica * CORES + core
    after = (replica, lax.rem(shard + 1, shards))
    before = (replica, lax.rem(shard + shards - 1, shards))

    def near_device(step):
        index = lax.rem(mine + step, near)
        return index, (lax.div(index, CORES), place * CORES + lax.rem(index, CORES))

    def far_device(step):
        index = lax.rem(place + step, places)
        return index, (replica, index * CORES + core)

    def z_device(step):
        return (lax.rem(replica + step, replicas), shard)

    def y_device(step):
        return (replica, (lax.rem(y + step, along_y) * ALONG_X + x) * CORES + core)

    def x_device(step):
        return (replica, (y * ALONG_X + lax.rem(x + step, ALONG_X)) * CORES + core)

    other_core = (replica, place * CORES + 1 - core)

    barrier = pltpu.get_barrier_semaphore()

    def signal(semaphore, device):
        pl.semaphore_signal(semaphore, inc=1, device_id=device, device_id_type=MESH)

    signal(barrier, before)
    signal(barrier, other_core)
    for step in range(1, ALONG_X):
        signal(barrier, x_device(step))
    for step in range(1, along_y):
        signal(barrier, y_device(step))
    for step in range(1, replicas):
        signal(barrier, z_device(step))

    loads = [
        (clip_hbm, clip),
        (res_hbm, res),
        (dest_hbm, dest),
        (bias_hbm, bias),
        (gain_hbm, gain),
        (head_bias_hbm, head_bias),
        (mean_hbm, mean),
        (scale_hbm, scale),
        (tconv_hbm, tconv),
        (head_hbm, head),
    ]
    for index in range(frame_count):
        pair = pl.ds(2 * index, 2)
        loads.append((frames_hbm.at[pair], frames.at[pair]))
    loads = [
        pltpu.make_async_copy(source, target, load_sem.at[index])
        for index, (source, target) in enumerate(loads)
    ]
    for load in loads:
        load.start()

    def patch_of(cell):
        row, column = lax.div(cell, columns), lax.rem(cell, columns)
        part = lax.rem(row, 2) * 2 + lax.rem(column, 2)
        return part * (cells // 4) + lax.div(row, 2) * (columns // 2) + lax.div(column, 2)

    def slot(row):
        rest = lax.rem(row, shards)
        return lax.div(rest, CORES) * near + lax.div(row, shards) * CORES + lax.rem(rest, CORES)

    unpatch[...] = reorder(cells, patch_of)
    turn[...] = reorder(total, lambda row: lax.rem(row, near) * places + lax.div(row, near))
    back[...] = reorder(total, slot)

    for load in loads[:8]:
        load.wait()
    first_frame = shard * frame_count
    first, one, two, limit = frame_facts(
        clip[...].astype(F32), res[...].astype(F32), first_frame, shards * frame_count, columns
    )
    row = iota((total, 1), 0)
    owner, spot = lax.div(row, places), lax.rem(row, places)
    named = lax.div(owner, CORES) * shards + spot * CORES + lax.rem(owner, CORES)
    tokens = dest.shape[1]
    matches = dest[...] == named
    match[...] = jnp.where(matches, 1.0, 0.0).astype(BF16)
    sooner = jnp.where(iota((tokens, tokens), 0) < iota((tokens, tokens), 1), 1.0, 0.0).astype(BF16)
    counts = jnp.dot(match[...], sooner, preferred_element_type=F32)
    rank = jnp.sum(jnp.where(matches, counts, 0.0), axis=0, keepdims=True)
    bias_row = bias[...].reshape(1, channels)
    gain_row = gain[...].reshape(1, channels)
    head_bias_column = column_of(head_bias[...])
    mean_column = column_of(mean[...])
    scale_column = column_of(scale[...])

    pl.semaphore_wait(barrier, 1 + 1 + ALONG_X - 1 + along_y - 1 + replicas - 1)
    rows = cells // CHUNKS
    sends = []
    for chunk in range(CHUNKS):
        part = pl.ds(chunk * rows, rows)
        sends.append(
            pltpu.make_async_remote_copy(
                src_ref=frames_hbm.at[2 * frame_count - 1, part],
                dst_ref=carried.at[part],
                send_sem=carry_send.at[chunk],
                recv_sem=carry_recv.at[chunk],
                device_id=after,
                device_id_type=MESH,
            )
        )
        sends[-1].start()
    signal(ready_sem, other_core)
    for step in range(1, ALONG_X):
        signal(ready_sem, x_device(step))

    for load in loads[8:]:
        load.wait()

    def section_frame(index, carry):
        taken = jnp.concatenate(
            [frames[2 * index - 1], frames[2 * index], frames[2 * index + 1]], axis=1
        )
        section[...] = jnp.dot(taken, tconv[...], preferred_element_type=F32)
        is_first, inside = pick(first, index), pick(limit, index)

        def part_of(chunk, carry):
            part = pl.ds(pl.multiple_of(chunk * rows, rows), rows)
            active[part, :] = activated(
                section[part, :] + bias_row,
                frames[2 * index + 1, part, :],
                is_first,
                gain_row,
                inside,
                columns,
            )
            return carry

        lax.fori_loop(0, CHUNKS, part_of, 0)
        products[index] = lax.dot_general(
            head[...], active[...], (((1,), (1,)), ((), ())), preferred_element_type=F32
        )
        return carry

    lax.fori_loop(1, frame_count, section_frame, 0)

    def tap_block(index, k):
        return products[index, k * taps : (k + 1) * taps]

    halo_out[0] = spatial_sum(
        tap_block(frame_count - 2, 0) * pick(two, frame_count)
        + tap_block(frame_count - 1, 1) * pick(one, frame_count),
        latent_dim,
        columns,
    )
    halo_out[1] = spatial_sum(
        tap_block(frame_count - 1, 0) * pick(two, frame_count + 1), latent_dim, columns
    )
    halo = pltpu.make_async_remote_copy(
        src_ref=halo_out,
        dst_ref=halo_in,
        send_sem=halo_sem.at[0],
        recv_sem=halo_sem.at[1],
        device_id=after,
        device_id_type=MESH,
    )
    halo.start()

    for index in range(1, frame_count):
        block = tap_block(index, 2)
        if index >= 2:
            block = block + tap_block(index - 1, 1) * pick(one, index)
        if index >= 3:
            block = block + tap_block(index - 2, 0) * pick(two, index)
        latents[index] = spatial_sum(block, latent_dim, columns)

    section[...] = jnp.dot(
        jnp.concatenate([frames[0], frames[1]], axis=1),
        tconv[channels:, :],
        preferred_element_type=F32,
    )
    is_first, inside = pick(first, 0), pick(limit, 0)
    for chunk in range(CHUNKS):
        part = pl.ds(chunk * rows, rows)
        sends[chunk].wait_recv()
        summed = section[part, :] + jnp.dot(
            carried[part, :], tconv[:channels, :], preferred_element_type=F32
        )
        act = activated(
            summed + bias_row, frames[1, part, :], is_first, gain_row, inside, columns
        )
        products[0, :, part] = lax.dot_general(
            head[...], act, (((1,), (1,)), ((), ())), preferred_element_type=F32
        )

    latents[0] = spatial_sum(tap_block(0, 2), latent_dim, columns)
    latents[1] += spatial_sum(tap_block(0, 1) * pick(one, 1), latent_dim, columns)
    latents[2] += spatial_sum(tap_block(0, 0) * pick(two, 2), latent_dim, columns)
    halo.wait_recv()
    latents[0] += halo_in[0]
    latents[1] += halo_in[1]
    column = lax.rem(iota((1, cells), 1), columns).astype(F32)
    finished = []
    for index in range(frame_count):
        inside = jnp.where(column < pick(limit, index), 1.0, 0.0)
        value = (latents[index] + head_bias_column - mean_column) * scale_column * inside
        finished.append(value.astype(BF16))
    parts = jnp.dot(
        jnp.concatenate(finished, axis=0), unpatch[...], preferred_element_type=F32
    )
    patch_count = cells // 4
    features = jnp.concatenate(
        [
            jnp.concatenate(
                [
                    parts[
                        index * latent_dim : (index + 1) * latent_dim,
                        quarter * patch_count : (quarter + 1) * patch_count,
                    ]
                    for index in range(frame_count)
                ],
                axis=1,
            )
            for quarter in range(4)
        ],
        axis=0,
    )
    ranked = jnp.concatenate(
        [jnp.where(rank == 0.0, features, 0.0), jnp.where(rank == 1.0, features, 0.0)], axis=0
    ).astype(BF16)
    outgoing[...] = lax.dot_general(
        match[...], ranked, (((1,), (1,)), ((), ())), preferred_element_type=F32
    ).astype(BF16)

    pl.semaphore_wait(ready_sem, 1 + ALONG_X - 1)

    def near_send(step, carry):
        index, device = near_device(step)
        pltpu.make_async_remote_copy(
            src_ref=outgoing.at[pl.ds(index * places, places)],
            dst_ref=first_stage.at[pl.ds(mine * places, places)],
            send_sem=send_sem.at[0],
            recv_sem=recv_sem.at[0],
            device_id=device,
            device_id_type=MESH,
        ).start()
        return carry

    lax.fori_loop(1, near, near_send, 0)
    own = pl.ds(mine * places, places)
    first_stage[own, :] = outgoing[own, :]
    arrived = first_stage.at[pl.ds(0, (near - 1) * places)]
    pltpu.make_async_copy(arrived, arrived, recv_sem.at[0]).wait()
    middle[...] = jnp.dot(turn[...], first_stage[...], preferred_element_type=F32).astype(BF16)

    def far_send(step, carry):
        index, device = far_device(step)
        pltpu.make_async_remote_copy(
            src_ref=middle.at[pl.ds(index * near, near)],
            dst_ref=last_stage.at[pl.ds(place * near, near)],
            send_sem=send_sem.at[1],
            recv_sem=recv_sem.at[1],
            device_id=device,
            device_id_type=MESH,
        ).start()
        return carry

    lax.fori_loop(1, places, far_send, 0)
    own = pl.ds(place * near, near)
    last_stage[own, :] = middle[own, :]
    for chunk in range(CHUNKS):
        sends[chunk].wait_send()
    halo.wait_send()
    sent = outgoing.at[pl.ds(0, (near - 1) * places)]
    pltpu.make_async_copy(sent, sent, send_sem.at[0]).wait()
    arrived = last_stage.at[pl.ds(0, (places - 1) * near)]
    pltpu.make_async_copy(arrived, arrived, recv_sem.at[1]).wait()
    out_ref[...] = jnp.dot(back[...], last_stage[...], preferred_element_type=F32)
    sent = middle.at[pl.ds(0, (places - 1) * near)]
    pltpu.make_async_copy(sent, sent, send_sem.at[1]).wait()


def on_device(
    replicas,
    shards,
    frames_in,
    clip_frames,
    res_ids,
    token_dest,
    tconv_weight,
    tconv_bias,
    head_gain,
    head_weight,
    head_bias,
    latent_mean,
    latent_scale,
):
    _, frame_count, slots, height, columns, channels = frames_in.shape
    latent_dim = head_weight.shape[-1]
    cells = height * columns
    tokens = token_dest.shape[1]
    clips = clip_frames.shape[1]
    destinations = replicas * shards
    width = 2 * 4 * latent_dim
    places = shards // CORES
    operands = (
        frames_in.reshape(frame_count * slots, cells, channels),
        clip_frames,
        res_ids,
        token_dest.reshape(1, tokens),
        tconv_weight.reshape(3 * channels, channels),
        tconv_bias,
        head_gain,
        jnp.transpose(head_weight, (0, 1, 2, 4, 3)).reshape(27 * latent_dim, channels),
        head_bias.reshape(1, latent_dim),
        latent_mean.reshape(1, latent_dim),
        latent_scale.reshape(1, latent_dim),
    )
    square = pltpu.VMEM((destinations, destinations), BF16)
    exchanged = pltpu.VMEM((destinations, width), BF16)
    slots_out = pl.pallas_call(
        functools.partial(encode_kernel, replicas, places, height, columns),
        out_shape=jax.ShapeDtypeStruct((destinations, width), F32),
        in_specs=[pl.BlockSpec(memory_space=pltpu.HBM)] * len(operands),
        out_specs=pl.BlockSpec(memory_space=pltpu.VMEM),
        scratch_shapes=[
            pltpu.VMEM(operand.shape, operand.dtype) for operand in operands
        ]
        + [
            pltpu.VMEM((cells, channels), BF16),
            pltpu.VMEM((2, latent_dim, cells), F32),
            pltpu.VMEM((2, latent_dim, cells), F32),
            pltpu.VMEM((cells, channels), F32),
            pltpu.VMEM((cells, channels), BF16),
            pltpu.VMEM((frame_count, 27 * latent_dim, cells), F32),
            pltpu.VMEM((frame_count, latent_dim, cells), F32),
            pltpu.VMEM((destinations, tokens), BF16),
            square,
            square,
            pltpu.VMEM((cells, cells), BF16),
            exchanged,
            exchanged,
            exchanged,
            exchanged,
            pltpu.SemaphoreType.DMA((10 + frame_count,)),
            pltpu.SemaphoreType.DMA((CHUNKS,)),
            pltpu.SemaphoreType.DMA((CHUNKS,)),
            pltpu.SemaphoreType.DMA((2,)),
            pltpu.SemaphoreType.REGULAR,
            pltpu.SemaphoreType.DMA((2,)),
            pltpu.SemaphoreType.DMA((2,)),
        ],
        compiler_params=pltpu.CompilerParams(
            collective_id=0, has_side_effects=True, vmem_limit_bytes=60 * 1024 * 1024
        ),
        name="encode_and_route",
    )(*operands)
    return slots_out.astype(BF16).reshape(1, 1, destinations, width)


def solution(mesh):
    in_specs = (
        P("dp", "seq", None, None, None, None),
        P("dp", None),
        P("dp", None),
        P("dp", "seq", None),
        P(),
        P(),
        P(),
        P(),
        P(),
        P(),
        P(),
    )
    out_specs = P("dp", "seq", None, None)
    return jax.shard_map(
        functools.partial(on_device, mesh.shape["dp"], mesh.shape["seq"]),
        mesh=mesh,
        in_specs=in_specs,
        out_specs=out_specs,
        check_vma=False,
    )
```

```python
import functools

import jax
import jax.numpy as jnp
from jax import lax
from jax.experimental import pallas as pl
from jax.experimental.pallas import tpu as pltpu
from jax.sharding import PartitionSpec as P

CORES = 2
ALONG_X = 4
CHUNKS = 2
MESH = pl.DeviceIdType.MESH
F32 = jnp.float32
BF16 = jnp.bfloat16


def iota(shape, axis):
    return lax.broadcasted_iota(jnp.int32, shape, axis)


def reorder(rows, source_of):
    source = source_of(iota((rows, 1), 0))
    return jnp.where(iota((rows, rows), 1) == source, 1.0, 0.0).astype(BF16)


def column_of(row):
    count = row.shape[1]
    diagonal = iota((count, count), 0) == iota((count, count), 1)
    return jnp.sum(jnp.where(diagonal, row, 0.0), axis=1, keepdims=True)


def frame_facts(lengths, resolutions, first_frame, total_frames, columns):
    clips = lengths.shape[1]
    earlier = iota((clips, clips), 1) < iota((clips, clips), 0)
    own = iota((clips, clips), 1) == iota((clips, clips), 0)
    starts = jnp.sum(jnp.where(earlier, lengths, 0.0), axis=1, keepdims=True)
    ends = starts + column_of(lengths)
    resolution = jnp.sum(jnp.where(own, resolutions, 0.0), axis=1, keepdims=True)
    frame = (first_frame + iota((clips, 128), 1)).astype(F32)
    belongs = (frame >= starts) & (frame < ends)
    start = jnp.sum(jnp.where(belongs, starts, 0.0), axis=0, keepdims=True)
    kind = jnp.sum(jnp.where(belongs, resolution, 0.0), axis=0, keepdims=True)
    frame = frame[:1]
    exists = frame < float(total_frames)
    first = jnp.where(frame == start, 1.0, 0.0)
    one = jnp.where((frame - 1.0 >= start) & exists, 1.0, 0.0)
    two = jnp.where((frame - 2.0 >= start) & exists, 1.0, 0.0)
    limit = jnp.where(kind == 1.0, float(columns), float(columns * 13 // 20))
    return first, one, two, limit


def pick(row, index):
    return jnp.sum(jnp.where(iota(row.shape, 1) == index, row, 0.0), axis=1, keepdims=True)


def spatial_sum(taps, latent_dim, columns):
    cells = taps.shape[1]
    band = 3 * latent_dim
    cell = iota((1, cells), 1)
    column = lax.rem(cell, columns)
    above = jnp.where(cell >= columns, pltpu.roll(taps[:band], columns, 1), 0.0)
    below = jnp.where(cell < cells - columns, pltpu.roll(taps[2 * band :], cells - columns, 1), 0.0)
    rows = taps[band : 2 * band] + above + below
    left = jnp.where(column >= 1, pltpu.roll(rows[:latent_dim], 1, 1), 0.0)
    right = jnp.where(column < columns - 1, pltpu.roll(rows[2 * latent_dim :], cells - 1, 1), 0.0)
    return rows[latent_dim : 2 * latent_dim] + left + right


def activated(section, passed, first, gain, limit, columns):
    rows, channels = section.shape
    section = jnp.where(first > 0.5, passed.astype(F32), section).astype(BF16).astype(F32)
    mean_square = jnp.sum(section * section, axis=1, keepdims=True) * (1.0 / channels)
    column = lax.rem(iota((rows, 1), 0), columns).astype(F32)
    inside = jnp.where(column < limit, 0.5, 0.0)
    half = section * (lax.rsqrt(mean_square + 1e-06) * 0.5) * gain
    return (half * 2.0 * (inside + inside * jnp.tanh(half))).astype(BF16)


def encode_kernel(
    replicas,
    places,
    height,
    columns,
    frames_hbm,
    clip_hbm,
    res_hbm,
    dest_hbm,
    tconv_hbm,
    bias_hbm,
    gain_hbm,
    head_hbm,
    head_bias_hbm,
    mean_hbm,
    scale_hbm,
    out_ref,
    frames,
    clip,
    res,
    dest,
    tconv,
    bias,
    gain,
    head,
    head_bias,
    mean,
    scale,
    carried,
    halo_in,
    halo_out,
    section,
    active,
    products,
    latents,
    match,
    turn,
    back,
    unpatch,
    outgoing,
    first_stage,
    middle,
    last_stage,
    load_sem,
    carry_send,
    carry_recv,
    halo_sem,
    ready_sem,
    send_sem,
    recv_sem,
):
    near = replicas * CORES
    total = near * places
    shards = places * CORES
    along_y = places // ALONG_X
    frame_count = frames.shape[0] // 2
    cells, channels = frames.shape[1:]
    latent_dim = head_bias.shape[1]
    taps = 9 * latent_dim
    replica = lax.axis_index("dp")
    shard = lax.axis_index("seq")
    place = lax.div(shard, CORES)
    core = lax.rem(shard, CORES)
    x = lax.rem(place, ALONG_X)
    y = lax.div(place, ALONG_X)
    mine = replica * CORES + core
    after = (replica, lax.rem(shard + 1, shards))
    before = (replica, lax.rem(shard + shards - 1, shards))

    def near_device(step):
        index = lax.rem(mine + step, near)
        return index, (lax.div(index, CORES), place * CORES + lax.rem(index, CORES))

    def far_device(step):
        index = lax.rem(place + step, places)
        return index, (replica, index * CORES + core)

    def z_device(step):
        return (lax.rem(replica + step + replicas, replicas), shard)

    def y_device(step):
        return (replica, (lax.rem(y + step + along_y, along_y) * ALONG_X + x) * CORES + core)

    def x_device(step):
        return (replica, (y * ALONG_X + lax.rem(x + step + ALONG_X, ALONG_X)) * CORES + core)

    other_core = (replica, place * CORES + 1 - core)

    barrier = pltpu.get_barrier_semaphore()

    def signal(semaphore, *devices):
        for device in devices:
            pl.semaphore_signal(semaphore, inc=1, device_id=device, device_id_type=MESH)

    signal(barrier, before, other_core, x_device(1), x_device(-1))
    signal(barrier, y_device(1), y_device(-1), z_device(1), z_device(-1))

    wanted = [(tconv_hbm, tconv)]
    wanted += [(frames_hbm.at[index], frames.at[index]) for index in (3, 4, 5, 6, 7)]
    wanted += [(head_hbm, head), (bias_hbm, bias), (gain_hbm, gain), (clip_hbm, clip), (res_hbm, res)]
    wanted += [(frames_hbm.at[index], frames.at[index]) for index in (2, 1, 0)]
    wanted += [(dest_hbm, dest), (head_bias_hbm, head_bias), (mean_hbm, mean), (scale_hbm, scale)]
    loads = [
        pltpu.make_async_copy(source, target, load_sem.at[index])
        for index, (source, target) in enumerate(wanted)
    ]
    for load in loads:
        load.start()

    def arrive(first_load, last_load):
        for load in loads[first_load : last_load + 1]:
            load.wait()

    def patch_of(cell):
        row, column = lax.div(cell, columns), lax.rem(cell, columns)
        part = lax.rem(row, 2) * 2 + lax.rem(column, 2)
        return part * (cells // 4) + lax.div(row, 2) * (columns // 2) + lax.div(column, 2)

    def slot(row):
        rest = lax.rem(row, shards)
        return lax.div(rest, CORES) * near + lax.div(row, shards) * CORES + lax.rem(rest, CORES)

    unpatch[...] = reorder(cells, patch_of)
    turn[...] = reorder(total, lambda row: lax.rem(row, near) * places + lax.div(row, near))
    back[...] = reorder(total, slot)


    rows = cells // CHUNKS
    sends = [
        pltpu.make_async_remote_copy(
            src_ref=frames_hbm.at[2 * frame_count - 1, pl.ds(chunk * rows, rows)],
            dst_ref=carried.at[pl.ds(chunk * rows, rows)],
            send_sem=carry_send.at[chunk],
            recv_sem=carry_recv.at[chunk],
            device_id=after,
            device_id_type=MESH,
        )
        for chunk in range(CHUNKS)
    ]
    pl.semaphore_wait(barrier, 8)
    for send in sends:
        send.start()
    signal(ready_sem.at[0], x_device(1), y_device(1), y_device(-1), z_device(1), z_device(-1))

    arrive(7, 10)
    first_frame = shard * frame_count
    first, one, two, limit = frame_facts(
        clip[...].astype(F32), res[...].astype(F32), first_frame, shards * frame_count, columns
    )
    bias_row = bias[...].reshape(1, channels)
    gain_row = gain[...].reshape(1, channels)

    def part_of(chunk):
        return slice(chunk * rows, (chunk + 1) * rows)

    def section_of(index, chunk, spot):
        part = part_of(chunk)
        taken = jnp.concatenate(
            [frames[2 * index - 1, part], frames[2 * index, part], frames[2 * index + 1, part]],
            axis=1,
        )
        section[spot] = jnp.dot(taken, tconv[...], preferred_element_type=F32)

    def activation_of(index, chunk, spot, target):
        active[target] = activated(
            section[spot] + bias_row,
            frames[2 * index + 1, part_of(chunk)],
            pick(first, index),
            gain_row,
            pick(limit, index),
            columns,
        )

    def products_of(index, chunk, target):
        products[index, :, part_of(chunk)] = lax.dot_general(
            head[...], active[target], (((1,), (1,)), ((), ())), preferred_element_type=F32
        )

    def tap_block(index, k):
        return products[index, k * taps : (k + 1) * taps]

    arrive(0, 3)
    units = [(index, chunk) for index in (2, 3, 1) for chunk in range(CHUNKS)]
    before_frame_3, before_frame_1 = CHUNKS, 2 * CHUNKS
    for step in range(len(units) + 2):
        if step == before_frame_3:
            arrive(4, 6)
            pl.semaphore_wait(ready_sem.at[0], 5)
            signal(ready_sem.at[1], y_device(2), y_device(-2), z_device(2), z_device(-2))
        if step == before_frame_1:
            arrive(11, 13)
            pl.semaphore_wait(ready_sem.at[1], 4)
            signal(ready_sem.at[2], other_core, x_device(1), x_device(2), x_device(-1))
        if step < len(units):
            section_of(*units[step], step % 2)
        if 1 <= step < len(units) + 1:
            activation_of(*units[step - 1], (step - 1) % 2, step % 2)
        if step >= 2:
            products_of(*units[step - 2], (step - 1) % 2)
        if step == before_frame_1 + 1:
            halo_out[0] = spatial_sum(
                tap_block(frame_count - 2, 0) * pick(two, frame_count)
                + tap_block(frame_count - 1, 1) * pick(one, frame_count),
                latent_dim,
                columns,
            )
            halo_out[1] = spatial_sum(
                tap_block(frame_count - 1, 0) * pick(two, frame_count + 1), latent_dim, columns
            )
            halo = pltpu.make_async_remote_copy(
                src_ref=halo_out,
                dst_ref=halo_in,
                send_sem=halo_sem.at[0],
                recv_sem=halo_sem.at[1],
                device_id=after,
                device_id_type=MESH,
            )
            halo.start()

    for chunk in range(CHUNKS):
        part = part_of(chunk)
        section[chunk % 2] = jnp.dot(
            jnp.concatenate([frames[0, part], frames[1, part]], axis=1),
            tconv[channels:, :],
            preferred_element_type=F32,
        )

    latents[1] = spatial_sum(tap_block(1, 2), latent_dim, columns)
    latents[2] = spatial_sum(tap_block(2, 2) + tap_block(1, 1) * pick(one, 2), latent_dim, columns)
    latents[3] = spatial_sum(
        tap_block(3, 2) + tap_block(2, 1) * pick(one, 3) + tap_block(1, 0) * pick(two, 3),
        latent_dim,
        columns,
    )

    arrive(14, 17)
    row = iota((total, 1), 0)
    owner, spot = lax.div(row, places), lax.rem(row, places)
    named = lax.div(owner, CORES) * shards + spot * CORES + lax.rem(owner, CORES)
    tokens = dest.shape[1]
    matches = dest[...] == named
    match[...] = jnp.where(matches, 1.0, 0.0).astype(BF16)
    sooner = jnp.where(iota((tokens, tokens), 0) < iota((tokens, tokens), 1), 1.0, 0.0).astype(BF16)
    counts = jnp.dot(match[...], sooner, preferred_element_type=F32)
    rank = jnp.sum(jnp.where(matches, counts, 0.0), axis=0, keepdims=True)
    head_bias_column = column_of(head_bias[...])
    mean_column = column_of(mean[...])
    scale_column = column_of(scale[...])

    for chunk in range(CHUNKS):
        part = part_of(chunk)
        sends[chunk].wait_recv()
        section[chunk % 2] += jnp.dot(
            carried[part, :], tconv[:channels, :], preferred_element_type=F32
        )
        activation_of(0, chunk, chunk % 2, chunk % 2)
        products_of(0, chunk, chunk % 2)

    latents[0] = spatial_sum(tap_block(0, 2), latent_dim, columns)
    latents[1] += spatial_sum(tap_block(0, 1) * pick(one, 1), latent_dim, columns)
    latents[2] += spatial_sum(tap_block(0, 0) * pick(two, 2), latent_dim, columns)
    halo.wait_recv()
    latents[0] += halo_in[0]
    latents[1] += halo_in[1]
    column = lax.rem(iota((1, cells), 1), columns).astype(F32)
    finished = []
    for index in range(frame_count):
        inside = jnp.where(column < pick(limit, index), 1.0, 0.0)
        value = (latents[index] + head_bias_column - mean_column) * scale_column * inside
        finished.append(value.astype(BF16))
    parts = jnp.dot(
        jnp.concatenate(finished, axis=0), unpatch[...], preferred_element_type=F32
    )
    patch_count = cells // 4
    features = jnp.concatenate(
        [
            jnp.concatenate(
                [
                    parts[
                        index * latent_dim : (index + 1) * latent_dim,
                        quarter * patch_count : (quarter + 1) * patch_count,
                    ]
                    for index in range(frame_count)
                ],
                axis=1,
            )
            for quarter in range(4)
        ],
        axis=0,
    )
    ranked = jnp.concatenate(
        [jnp.where(rank == 0.0, features, 0.0), jnp.where(rank == 1.0, features, 0.0)], axis=0
    ).astype(BF16)
    outgoing[...] = lax.dot_general(
        match[...], ranked, (((1,), (1,)), ((), ())), preferred_element_type=F32
    ).astype(BF16)

    pl.semaphore_wait(ready_sem.at[2], 4)

    def near_send(step, carry):
        index, device = near_device(step)
        pltpu.make_async_remote_copy(
            src_ref=outgoing.at[pl.ds(index * places, places)],
            dst_ref=first_stage.at[pl.ds(mine * places, places)],
            send_sem=send_sem.at[0],
            recv_sem=recv_sem.at[0],
            device_id=device,
            device_id_type=MESH,
        ).start()
        return carry

    lax.fori_loop(1, near, near_send, 0)
    own = pl.ds(mine * places, places)
    first_stage[own, :] = outgoing[own, :]
    arrived = first_stage.at[pl.ds(0, (near - 1) * places)]
    pltpu.make_async_copy(arrived, arrived, recv_sem.at[0]).wait()
    middle[...] = jnp.dot(turn[...], first_stage[...], preferred_element_type=F32).astype(BF16)

    def far_send(step, carry):
        index, device = far_device(step)
        pltpu.make_async_remote_copy(
            src_ref=middle.at[pl.ds(index * near, near)],
            dst_ref=last_stage.at[pl.ds(place * near, near)],
            send_sem=send_sem.at[1],
            recv_sem=recv_sem.at[1],
            device_id=device,
            device_id_type=MESH,
        ).start()
        return carry

    lax.fori_loop(1, places, far_send, 0)
    own = pl.ds(place * near, near)
    last_stage[own, :] = middle[own, :]
    for chunk in range(CHUNKS):
        sends[chunk].wait_send()
    halo.wait_send()
    sent = outgoing.at[pl.ds(0, (near - 1) * places)]
    pltpu.make_async_copy(sent, sent, send_sem.at[0]).wait()
    arrived = last_stage.at[pl.ds(0, (places - 1) * near)]
    pltpu.make_async_copy(arrived, arrived, recv_sem.at[1]).wait()
    out_ref[...] = jnp.dot(back[...], last_stage[...], preferred_element_type=F32)
    sent = middle.at[pl.ds(0, (places - 1) * near)]
    pltpu.make_async_copy(sent, sent, send_sem.at[1]).wait()


def on_device(
    replicas,
    shards,
    frames_in,
    clip_frames,
    res_ids,
    token_dest,
    tconv_weight,
    tconv_bias,
    head_gain,
    head_weight,
    head_bias,
    latent_mean,
    latent_scale,
):
    _, frame_count, slots, height, columns, channels = frames_in.shape
    latent_dim = head_weight.shape[-1]
    cells = height * columns
    tokens = token_dest.shape[1]
    clips = clip_frames.shape[1]
    destinations = replicas * shards
    width = 2 * 4 * latent_dim
    places = shards // CORES
    operands = (
        frames_in.reshape(frame_count * slots, cells, channels),
        clip_frames,
        res_ids,
        token_dest.reshape(1, tokens),
        tconv_weight.reshape(3 * channels, channels),
        tconv_bias,
        head_gain,
        jnp.transpose(head_weight, (0, 1, 2, 4, 3)).reshape(27 * latent_dim, channels),
        head_bias.reshape(1, latent_dim),
        latent_mean.reshape(1, latent_dim),
        latent_scale.reshape(1, latent_dim),
    )
    square = pltpu.VMEM((destinations, destinations), BF16)
    exchanged = pltpu.VMEM((destinations, width), BF16)
    slots_out = pl.pallas_call(
        functools.partial(encode_kernel, replicas, places, height, columns),
        out_shape=pltpu.VMEM((destinations, width), F32),
        in_specs=[pl.BlockSpec(memory_space=pltpu.HBM)] * len(operands),
        out_specs=pl.BlockSpec(memory_space=pltpu.VMEM),
        scratch_shapes=[
            pltpu.VMEM(operand.shape, operand.dtype) for operand in operands
        ]
        + [
            pltpu.VMEM((cells, channels), BF16),
            pltpu.VMEM((2, latent_dim, cells), F32),
            pltpu.VMEM((2, latent_dim, cells), F32),
            pltpu.VMEM((2, cells // CHUNKS, channels), F32),
            pltpu.VMEM((2, cells // CHUNKS, channels), BF16),
            pltpu.VMEM((frame_count, 27 * latent_dim, cells), F32),
            pltpu.VMEM((frame_count, latent_dim, cells), F32),
            pltpu.VMEM((destinations, tokens), BF16),
            square,
            square,
            pltpu.VMEM((cells, cells), BF16),
            exchanged,
            exchanged,
            exchanged,
            exchanged,
            pltpu.SemaphoreType.DMA((10 + 2 * frame_count,)),
            pltpu.SemaphoreType.DMA((CHUNKS,)),
            pltpu.SemaphoreType.DMA((CHUNKS,)),
            pltpu.SemaphoreType.DMA((2,)),
            pltpu.SemaphoreType.REGULAR((3,)),
            pltpu.SemaphoreType.DMA((2,)),
            pltpu.SemaphoreType.DMA((2,)),
        ],
        compiler_params=pltpu.CompilerParams(
            collective_id=0, has_side_effects=True, vmem_limit_bytes=60 * 1024 * 1024
        ),
        name="encode_and_route",
    )(*operands)
    return slots_out.astype(BF16).reshape(1, 1, destinations, width)


def solution(mesh):
    in_specs = (
        P("dp", "seq", None, None, None, None),
        P("dp", None),
        P("dp", None),
        P("dp", "seq", None),
        P(),
        P(),
        P(),
        P(),
        P(),
        P(),
        P(),
    )
    out_specs = P("dp", "seq", None, None)
    return jax.shard_map(
        functools.partial(on_device, mesh.shape["dp"], mesh.shape["seq"]),
        mesh=mesh,
        in_specs=in_specs,
        out_specs=out_specs,
        check_vma=False,
    )
```

```python
import functools

import jax
import jax.numpy as jnp
from jax import lax
from jax.experimental import pallas as pl
from jax.experimental.pallas import tpu as pltpu
from jax.sharding import PartitionSpec as P

CORES = 2
ALONG_X = 4
CHUNKS = 2
MESH = pl.DeviceIdType.MESH
F32 = jnp.float32
BF16 = jnp.bfloat16


def iota(shape, axis):
    return lax.broadcasted_iota(jnp.int32, shape, axis)


def reorder(rows, source_of):
    source = source_of(iota((rows, 1), 0))
    return jnp.where(iota((rows, rows), 1) == source, 1.0, 0.0).astype(BF16)


def column_of(row):
    count = row.shape[1]
    diagonal = iota((count, count), 0) == iota((count, count), 1)
    return jnp.sum(jnp.where(diagonal, row, 0.0), axis=1, keepdims=True)


def frame_facts(lengths, resolutions, first_frame, total_frames, columns):
    clips = lengths.shape[1]
    earlier = iota((clips, clips), 1) < iota((clips, clips), 0)
    own = iota((clips, clips), 1) == iota((clips, clips), 0)
    starts = jnp.sum(jnp.where(earlier, lengths, 0.0), axis=1, keepdims=True)
    ends = starts + column_of(lengths)
    resolution = jnp.sum(jnp.where(own, resolutions, 0.0), axis=1, keepdims=True)
    frame = (first_frame + iota((clips, 128), 1)).astype(F32)
    belongs = (frame >= starts) & (frame < ends)
    start = jnp.sum(jnp.where(belongs, starts, 0.0), axis=0, keepdims=True)
    kind = jnp.sum(jnp.where(belongs, resolution, 0.0), axis=0, keepdims=True)
    frame = frame[:1]
    exists = frame < float(total_frames)
    first = jnp.where(frame == start, 1.0, 0.0)
    one = jnp.where((frame - 1.0 >= start) & exists, 1.0, 0.0)
    two = jnp.where((frame - 2.0 >= start) & exists, 1.0, 0.0)
    limit = jnp.where(kind == 1.0, float(columns), float(columns * 13 // 20))
    return first, one, two, limit


def pick(row, index):
    return jnp.sum(jnp.where(iota(row.shape, 1) == index, row, 0.0), axis=1, keepdims=True)


def spatial_sum(taps, latent_dim, columns):
    cells = taps.shape[1]
    band = 3 * latent_dim
    cell = iota((1, cells), 1)
    column = lax.rem(cell, columns)
    above = jnp.where(cell >= columns, pltpu.roll(taps[:band], columns, 1), 0.0)
    below = jnp.where(cell < cells - columns, pltpu.roll(taps[2 * band :], cells - columns, 1), 0.0)
    rows = taps[band : 2 * band] + above + below
    left = jnp.where(column >= 1, pltpu.roll(rows[:latent_dim], 1, 1), 0.0)
    right = jnp.where(column < columns - 1, pltpu.roll(rows[2 * latent_dim :], cells - 1, 1), 0.0)
    return rows[latent_dim : 2 * latent_dim] + left + right


def activated(section, passed, first, gain, limit, columns):
    rows, channels = section.shape
    section = jnp.where(first > 0.5, passed.astype(F32), section).astype(BF16).astype(F32)
    mean_square = jnp.sum(section * section, axis=1, keepdims=True) * (1.0 / channels)
    column = lax.rem(iota((rows, 1), 0), columns).astype(F32)
    inside = jnp.where(column < limit, 0.5, 0.0)
    half = section * (lax.rsqrt(mean_square + 1e-06) * 0.5) * gain
    return (half * 2.0 * (inside + inside * jnp.tanh(half))).astype(BF16)


def encode_kernel(
    replicas,
    places,
    height,
    columns,
    frames_hbm,
    clip_hbm,
    res_hbm,
    dest_hbm,
    tconv_hbm,
    bias_hbm,
    gain_hbm,
    head_hbm,
    head_bias_hbm,
    mean_hbm,
    scale_hbm,
    out_ref,
    frames,
    clip,
    res,
    dest,
    tconv,
    bias,
    gain,
    head,
    head_bias,
    mean,
    scale,
    carried,
    halo_in,
    halo_out,
    section,
    active,
    products,
    latents,
    match,
    unpatch,
    outgoing,
    load_sem,
    carry_send,
    carry_recv,
    halo_sem,
    ready_sem,
    send_sem,
    recv_sem,
):
    shards = places * CORES
    total = replicas * shards
    line = ALONG_X * CORES
    along_y = places // ALONG_X
    frame_count = frames.shape[0] // 2
    cells, channels = frames.shape[1:]
    latent_dim = head_bias.shape[1]
    taps = 9 * latent_dim
    replica = lax.axis_index("dp")
    shard = lax.axis_index("seq")
    place = lax.div(shard, CORES)
    core = lax.rem(shard, CORES)
    x = lax.rem(place, ALONG_X)
    y = lax.div(place, ALONG_X)
    mine = replica * shards + shard
    after = (replica, lax.rem(shard + 1, shards))
    before = (replica, lax.rem(shard + shards - 1, shards))

    def z_device(step):
        return (lax.rem(replica + step + replicas, replicas), shard)

    def y_device(step):
        return (replica, (lax.rem(y + step + along_y, along_y) * ALONG_X + x) * CORES + core)

    def x_device(step):
        return (replica, (y * ALONG_X + lax.rem(x + step + ALONG_X, ALONG_X)) * CORES + core)

    other_core = (replica, place * CORES + 1 - core)

    barrier = pltpu.get_barrier_semaphore()

    def signal(semaphore, *devices):
        for device in devices:
            pl.semaphore_signal(semaphore, inc=1, device_id=device, device_id_type=MESH)

    signal(barrier, before, other_core, x_device(1), x_device(-1))
    signal(barrier, y_device(1), y_device(-1), z_device(1), z_device(-1))

    wanted = [(tconv_hbm, tconv)]
    wanted += [(frames_hbm.at[index], frames.at[index]) for index in (3, 4, 5, 6, 7)]
    wanted += [(head_hbm, head), (bias_hbm, bias), (gain_hbm, gain), (clip_hbm, clip), (res_hbm, res)]
    wanted += [(frames_hbm.at[index], frames.at[index]) for index in (2, 1, 0)]
    wanted += [(dest_hbm, dest), (head_bias_hbm, head_bias), (mean_hbm, mean), (scale_hbm, scale)]
    loads = [
        pltpu.make_async_copy(source, target, load_sem.at[index])
        for index, (source, target) in enumerate(wanted)
    ]
    for load in loads:
        load.start()

    def arrive(first_load, last_load):
        for load in loads[first_load : last_load + 1]:
            load.wait()

    def patch_of(cell):
        row, column = lax.div(cell, columns), lax.rem(cell, columns)
        part = lax.rem(row, 2) * 2 + lax.rem(column, 2)
        return part * (cells // 4) + lax.div(row, 2) * (columns // 2) + lax.div(column, 2)

    unpatch[...] = reorder(cells, patch_of)


    rows = cells // CHUNKS
    sends = [
        pltpu.make_async_remote_copy(
            src_ref=frames_hbm.at[2 * frame_count - 1, pl.ds(chunk * rows, rows)],
            dst_ref=carried.at[pl.ds(chunk * rows, rows)],
            send_sem=carry_send.at[chunk],
            recv_sem=carry_recv.at[chunk],
            device_id=after,
            device_id_type=MESH,
        )
        for chunk in range(CHUNKS)
    ]
    pl.semaphore_wait(barrier, 8)
    for send in sends:
        send.start()
    signal(ready_sem.at[0], x_device(1), y_device(1), y_device(-1), z_device(1), z_device(-1))

    arrive(7, 10)
    first_frame = shard * frame_count
    first, one, two, limit = frame_facts(
        clip[...].astype(F32), res[...].astype(F32), first_frame, shards * frame_count, columns
    )
    bias_row = bias[...].reshape(1, channels)
    gain_row = gain[...].reshape(1, channels)

    def part_of(chunk):
        return slice(chunk * rows, (chunk + 1) * rows)

    def section_of(index, chunk, spot):
        part = part_of(chunk)
        taken = jnp.concatenate(
            [frames[2 * index - 1, part], frames[2 * index, part], frames[2 * index + 1, part]],
            axis=1,
        )
        section[spot] = jnp.dot(taken, tconv[...], preferred_element_type=F32)

    def activation_of(index, chunk, spot, target):
        active[target] = activated(
            section[spot] + bias_row,
            frames[2 * index + 1, part_of(chunk)],
            pick(first, index),
            gain_row,
            pick(limit, index),
            columns,
        )

    def products_of(index, chunk, target):
        products[index, :, part_of(chunk)] = lax.dot_general(
            head[...], active[target], (((1,), (1,)), ((), ())), preferred_element_type=F32
        )

    def tap_block(index, k):
        return products[index, k * taps : (k + 1) * taps]

    arrive(0, 3)
    units = [(index, chunk) for index in (2, 3, 1) for chunk in range(CHUNKS)]
    before_frame_3, before_frame_1 = CHUNKS, 2 * CHUNKS
    for step in range(len(units) + 2):
        if step == before_frame_3:
            arrive(4, 6)
            pl.semaphore_wait(ready_sem.at[0], 5)
            signal(ready_sem.at[1], y_device(2), y_device(-2), z_device(2), z_device(-2))
        if step == before_frame_1:
            arrive(11, 13)
            pl.semaphore_wait(ready_sem.at[1], 4)
            signal(ready_sem.at[2], other_core)
        if step < len(units):
            section_of(*units[step], step % 2)
        if 1 <= step < len(units) + 1:
            activation_of(*units[step - 1], (step - 1) % 2, step % 2)
        if step >= 2:
            products_of(*units[step - 2], (step - 1) % 2)
        if step == before_frame_1 + 1:
            pl.semaphore_wait(ready_sem.at[2], 1)
            signal(ready_sem.at[3], *[y_device(step) for step in range(1, along_y)])
            halo_out[0] = spatial_sum(
                tap_block(frame_count - 2, 0) * pick(two, frame_count)
                + tap_block(frame_count - 1, 1) * pick(one, frame_count),
                latent_dim,
                columns,
            )
            halo_out[1] = spatial_sum(
                tap_block(frame_count - 1, 0) * pick(two, frame_count + 1), latent_dim, columns
            )
            halo = pltpu.make_async_remote_copy(
                src_ref=halo_out,
                dst_ref=halo_in,
                send_sem=halo_sem.at[0],
                recv_sem=halo_sem.at[1],
                device_id=after,
                device_id_type=MESH,
            )
            halo.start()

    for chunk in range(CHUNKS):
        part = part_of(chunk)
        section[chunk % 2] = jnp.dot(
            jnp.concatenate([frames[0, part], frames[1, part]], axis=1),
            tconv[channels:, :],
            preferred_element_type=F32,
        )

    latents[1] = spatial_sum(tap_block(1, 2), latent_dim, columns)
    latents[2] = spatial_sum(tap_block(2, 2) + tap_block(1, 1) * pick(one, 2), latent_dim, columns)
    latents[3] = spatial_sum(
        tap_block(3, 2) + tap_block(2, 1) * pick(one, 3) + tap_block(1, 0) * pick(two, 3),
        latent_dim,
        columns,
    )

    arrive(14, 17)
    tokens = dest.shape[1]
    matches = dest[...] == iota((total, 1), 0)
    match[...] = jnp.where(matches, 1.0, 0.0).astype(BF16)
    sooner = jnp.where(iota((tokens, tokens), 0) < iota((tokens, tokens), 1), 1.0, 0.0).astype(BF16)
    counts = jnp.dot(match[...], sooner, preferred_element_type=F32)
    rank = jnp.sum(jnp.where(matches, counts, 0.0), axis=0, keepdims=True)
    head_bias_column = column_of(head_bias[...])
    mean_column = column_of(mean[...])
    scale_column = column_of(scale[...])

    pl.semaphore_wait(ready_sem.at[3], along_y - 1)
    signal(ready_sem.at[4], x_device(1), x_device(2), x_device(-1))

    for chunk in range(CHUNKS):
        part = part_of(chunk)
        sends[chunk].wait_recv()
        section[chunk % 2] += jnp.dot(
            carried[part, :], tconv[:channels, :], preferred_element_type=F32
        )
        activation_of(0, chunk, chunk % 2, chunk % 2)
        products_of(0, chunk, chunk % 2)

    latents[0] = spatial_sum(tap_block(0, 2), latent_dim, columns)
    latents[1] += spatial_sum(tap_block(0, 1) * pick(one, 1), latent_dim, columns)
    latents[2] += spatial_sum(tap_block(0, 0) * pick(two, 2), latent_dim, columns)
    halo.wait_recv()
    latents[0] += halo_in[0]
    latents[1] += halo_in[1]
    column = lax.rem(iota((1, cells), 1), columns).astype(F32)
    finished = []
    for index in range(frame_count):
        inside = jnp.where(column < pick(limit, index), 1.0, 0.0)
        value = (latents[index] + head_bias_column - mean_column) * scale_column * inside
        finished.append(value.astype(BF16))
    parts = jnp.dot(
        jnp.concatenate(finished, axis=0), unpatch[...], preferred_element_type=F32
    )
    patch_count = cells // 4
    features = jnp.concatenate(
        [
            jnp.concatenate(
                [
                    parts[
                        index * latent_dim : (index + 1) * latent_dim,
                        quarter * patch_count : (quarter + 1) * patch_count,
                    ]
                    for index in range(frame_count)
                ],
                axis=1,
            )
            for quarter in range(4)
        ],
        axis=0,
    )
    ranked = jnp.concatenate(
        [jnp.where(rank == 0.0, features, 0.0), jnp.where(rank == 1.0, features, 0.0)], axis=0
    ).astype(BF16)
    outgoing[...] = lax.dot_general(
        match[...], ranked, (((1,), (1,)), ((), ())), preferred_element_type=F32
    )

    pl.semaphore_wait(ready_sem.at[4], ALONG_X - 1)

    def send_row(to_replica, to_shard):
        pltpu.make_async_remote_copy(
            src_ref=outgoing.at[pl.ds(to_replica * shards + to_shard, 1)],
            dst_ref=out_ref.at[pl.ds(mine, 1)],
            send_sem=send_sem,
            recv_sem=recv_sem,
            device_id=(to_replica, to_shard),
            device_id_type=MESH,
        ).start()

    def hops(offset):
        far_z, far_y = offset
        return min(far_z, replicas - far_z) + min(far_y, along_y - far_y)

    offsets = [(far_z, far_y) for far_z in range(replicas) for far_y in range(along_y)]
    for far_z, far_y in sorted(offsets, key=hops, reverse=True):
        to_replica = lax.rem(replica + far_z, replicas)
        to_line = lax.rem(y + far_y, along_y) * line

        def send_line(step, carry, to_replica=to_replica, to_line=to_line):
            send_row(to_replica, to_line + lax.rem(x * CORES + core + step, line))
            return carry

        lax.fori_loop(0 if far_z or far_y else 1, line, send_line, 0, unroll=True)

    out_ref[pl.ds(mine, 1), :] = outgoing[pl.ds(mine, 1), :]
    for send in sends:
        send.wait_send()
    halo.wait_send()
    others = out_ref.at[pl.ds(0, total - 1)]
    pltpu.make_async_copy(others, others, recv_sem).wait()
    others = outgoing.at[pl.ds(0, total - 1)]
    pltpu.make_async_copy(others, others, send_sem).wait()


def on_device(
    replicas,
    shards,
    frames_in,
    clip_frames,
    res_ids,
    token_dest,
    tconv_weight,
    tconv_bias,
    head_gain,
    head_weight,
    head_bias,
    latent_mean,
    latent_scale,
):
    _, frame_count, slots, height, columns, channels = frames_in.shape
    latent_dim = head_weight.shape[-1]
    cells = height * columns
    tokens = token_dest.shape[1]
    clips = clip_frames.shape[1]
    destinations = replicas * shards
    width = 2 * 4 * latent_dim
    places = shards // CORES
    operands = (
        frames_in.reshape(frame_count * slots, cells, channels),
        clip_frames,
        res_ids,
        token_dest.reshape(1, tokens),
        tconv_weight.reshape(3 * channels, channels),
        tconv_bias,
        head_gain,
        jnp.transpose(head_weight, (0, 1, 2, 4, 3)).reshape(27 * latent_dim, channels),
        head_bias.reshape(1, latent_dim),
        latent_mean.reshape(1, latent_dim),
        latent_scale.reshape(1, latent_dim),
    )
    slots_out = pl.pallas_call(
        functools.partial(encode_kernel, replicas, places, height, columns),
        out_shape=pltpu.VMEM((destinations, width), F32),
        in_specs=[pl.BlockSpec(memory_space=pltpu.HBM)] * len(operands),
        out_specs=pl.BlockSpec(memory_space=pltpu.VMEM),
        scratch_shapes=[
            pltpu.VMEM(operand.shape, operand.dtype) for operand in operands
        ]
        + [
            pltpu.VMEM((cells, channels), BF16),
            pltpu.VMEM((2, latent_dim, cells), F32),
            pltpu.VMEM((2, latent_dim, cells), F32),
            pltpu.VMEM((2, cells // CHUNKS, channels), F32),
            pltpu.VMEM((2, cells // CHUNKS, channels), BF16),
            pltpu.VMEM((frame_count, 27 * latent_dim, cells), F32),
            pltpu.VMEM((frame_count, latent_dim, cells), F32),
            pltpu.VMEM((destinations, tokens), BF16),
            pltpu.VMEM((cells, cells), BF16),
            pltpu.VMEM((destinations, width), F32),
            pltpu.SemaphoreType.DMA((10 + 2 * frame_count,)),
            pltpu.SemaphoreType.DMA((CHUNKS,)),
            pltpu.SemaphoreType.DMA((CHUNKS,)),
            pltpu.SemaphoreType.DMA((2,)),
            pltpu.SemaphoreType.REGULAR((5,)),
            pltpu.SemaphoreType.DMA,
            pltpu.SemaphoreType.DMA,
        ],
        compiler_params=pltpu.CompilerParams(
            collective_id=0, has_side_effects=True, vmem_limit_bytes=60 * 1024 * 1024
        ),
        name="encode_and_route",
    )(*operands)
    return slots_out.astype(BF16).reshape(1, 1, destinations, width)


def solution(mesh):
    in_specs = (
        P("dp", "seq", None, None, None, None),
        P("dp", None),
        P("dp", None),
        P("dp", "seq", None),
        P(),
        P(),
        P(),
        P(),
        P(),
        P(),
        P(),
    )
    out_specs = P("dp", "seq", None, None)
    return jax.shard_map(
        functools.partial(on_device, mesh.shape["dp"], mesh.shape["seq"]),
        mesh=mesh,
        in_specs=in_specs,
        out_specs=out_specs,
        check_vma=False,
    )
```

```python
import functools

import jax
import jax.numpy as jnp
from jax import lax
from jax.experimental import pallas as pl
from jax.experimental.pallas import tpu as pltpu
from jax.sharding import PartitionSpec as P

CORES = 2
ALONG_X = 4
CHUNKS = 2
MESH = pl.DeviceIdType.MESH
F32 = jnp.float32
BF16 = jnp.bfloat16


def iota(shape, axis):
    return lax.broadcasted_iota(jnp.int32, shape, axis)


def reorder(rows, source_of):
    source = source_of(iota((rows, 1), 0))
    return jnp.where(iota((rows, rows), 1) == source, 1.0, 0.0).astype(BF16)


def column_of(row):
    count = row.shape[1]
    diagonal = iota((count, count), 0) == iota((count, count), 1)
    return jnp.sum(jnp.where(diagonal, row, 0.0), axis=1, keepdims=True)


def frame_facts(lengths, resolutions, first_frame, total_frames, columns):
    clips = lengths.shape[1]
    earlier = iota((clips, clips), 1) < iota((clips, clips), 0)
    own = iota((clips, clips), 1) == iota((clips, clips), 0)
    starts = jnp.sum(jnp.where(earlier, lengths, 0.0), axis=1, keepdims=True)
    ends = starts + column_of(lengths)
    resolution = jnp.sum(jnp.where(own, resolutions, 0.0), axis=1, keepdims=True)
    frame = (first_frame + iota((clips, 128), 1)).astype(F32)
    belongs = (frame >= starts) & (frame < ends)
    start = jnp.sum(jnp.where(belongs, starts, 0.0), axis=0, keepdims=True)
    kind = jnp.sum(jnp.where(belongs, resolution, 0.0), axis=0, keepdims=True)
    frame = frame[:1]
    exists = frame < float(total_frames)
    first = jnp.where(frame == start, 1.0, 0.0)
    one = jnp.where((frame - 1.0 >= start) & exists, 1.0, 0.0)
    two = jnp.where((frame - 2.0 >= start) & exists, 1.0, 0.0)
    limit = jnp.where(kind == 1.0, float(columns), float(columns * 13 // 20))
    return first, one, two, limit


def pick(row, index):
    return jnp.sum(jnp.where(iota(row.shape, 1) == index, row, 0.0), axis=1, keepdims=True)


def spatial_sum(taps, latent_dim, columns):
    cells = taps.shape[1]
    band = 3 * latent_dim
    cell = iota((1, cells), 1)
    column = lax.rem(cell, columns)
    above = jnp.where(cell >= columns, pltpu.roll(taps[:band], columns, 1), 0.0)
    below = jnp.where(cell < cells - columns, pltpu.roll(taps[2 * band :], cells - columns, 1), 0.0)
    rows = taps[band : 2 * band] + above + below
    left = jnp.where(column >= 1, pltpu.roll(rows[:latent_dim], 1, 1), 0.0)
    right = jnp.where(column < columns - 1, pltpu.roll(rows[2 * latent_dim :], cells - 1, 1), 0.0)
    return rows[latent_dim : 2 * latent_dim] + left + right


def activated(section, passed, first, gain, limit, columns):
    rows, channels = section.shape
    section = jnp.where(first > 0.5, passed.astype(F32), section).astype(BF16).astype(F32)
    mean_square = jnp.sum(section * section, axis=1, keepdims=True) * (1.0 / channels)
    column = lax.rem(iota((rows, 1), 0), columns).astype(F32)
    inside = jnp.where(column < limit, 0.5, 0.0)
    half = section * (lax.rsqrt(mean_square + 1e-06) * 0.5) * gain
    return (half * 2.0 * (inside + inside * jnp.tanh(half))).astype(BF16)


def encode_kernel(
    replicas,
    places,
    height,
    columns,
    frames_hbm,
    clip_hbm,
    res_hbm,
    dest_hbm,
    tconv_hbm,
    bias_hbm,
    gain_hbm,
    head_hbm,
    head_bias_hbm,
    mean_hbm,
    scale_hbm,
    out_ref,
    frames,
    clip,
    res,
    dest,
    tconv,
    bias,
    gain,
    head,
    head_bias,
    mean,
    scale,
    carried,
    halo_in,
    halo_out,
    section,
    active,
    products,
    latents,
    match,
    unpatch,
    pairing,
    handed,
    taken,
    outgoing,
    load_sem,
    carry_send,
    carry_recv,
    halo_sem,
    ready_sem,
    swap_sem,
    home_sem,
    send_sem,
    recv_sem,
):
    shards = places * CORES
    total = replicas * shards
    along_y = places // ALONG_X
    frame_count = frames.shape[0] // 2
    cells, channels = frames.shape[1:]
    latent_dim = head_bias.shape[1]
    taps = 9 * latent_dim
    replica = lax.axis_index("dp")
    shard = lax.axis_index("seq")
    place = lax.div(shard, CORES)
    core = lax.rem(shard, CORES)
    x = lax.rem(place, ALONG_X)
    y = lax.div(place, ALONG_X)
    after = (replica, lax.rem(shard + 1, shards))
    before = (replica, lax.rem(shard + shards - 1, shards))

    def z_device(step):
        return (lax.rem(replica + step + replicas, replicas), shard)

    def y_device(step):
        return (replica, (lax.rem(y + step + along_y, along_y) * ALONG_X + x) * CORES + core)

    def x_device(step):
        return (replica, (y * ALONG_X + lax.rem(x + step + ALONG_X, ALONG_X)) * CORES + core)

    other_core = (replica, place * CORES + 1 - core)

    barrier = pltpu.get_barrier_semaphore()

    def signal(semaphore, *devices):
        for device in devices:
            pl.semaphore_signal(semaphore, inc=1, device_id=device, device_id_type=MESH)

    signal(barrier, before, other_core, x_device(1), x_device(-1))
    signal(barrier, y_device(1), y_device(-1), z_device(1), z_device(-1))

    wanted = [(tconv_hbm, tconv)]
    wanted += [(frames_hbm.at[index], frames.at[index]) for index in (3, 4, 5, 6, 7)]
    wanted += [(head_hbm, head), (bias_hbm, bias), (gain_hbm, gain), (clip_hbm, clip), (res_hbm, res)]
    wanted += [(frames_hbm.at[index], frames.at[index]) for index in (2, 1, 0)]
    wanted += [(dest_hbm, dest), (head_bias_hbm, head_bias), (mean_hbm, mean), (scale_hbm, scale)]
    loads = [
        pltpu.make_async_copy(source, target, load_sem.at[index])
        for index, (source, target) in enumerate(wanted)
    ]
    for load in loads:
        load.start()

    def arrive(first_load, last_load):
        for load in loads[first_load : last_load + 1]:
            load.wait()

    def patch_of(cell):
        row, column = lax.div(cell, columns), lax.rem(cell, columns)
        part = lax.rem(row, 2) * 2 + lax.rem(column, 2)
        return part * (cells // 4) + lax.div(row, 2) * (columns // 2) + lax.div(column, 2)

    unpatch[...] = reorder(cells, patch_of)


    rows = cells // CHUNKS
    sends = [
        pltpu.make_async_remote_copy(
            src_ref=frames_hbm.at[2 * frame_count - 1, pl.ds(chunk * rows, rows)],
            dst_ref=carried.at[pl.ds(chunk * rows, rows)],
            send_sem=carry_send.at[chunk],
            recv_sem=carry_recv.at[chunk],
            device_id=after,
            device_id_type=MESH,
        )
        for chunk in range(CHUNKS)
    ]
    pl.semaphore_wait(barrier, 8)
    for send in sends:
        send.start()
    signal(ready_sem.at[0], x_device(1), y_device(1), y_device(-1), z_device(1), z_device(-1))

    arrive(7, 10)
    first_frame = shard * frame_count
    first, one, two, limit = frame_facts(
        clip[...].astype(F32), res[...].astype(F32), first_frame, shards * frame_count, columns
    )
    bias_row = bias[...].reshape(1, channels)
    gain_row = gain[...].reshape(1, channels)

    def part_of(chunk):
        return slice(chunk * rows, (chunk + 1) * rows)

    def section_of(index, chunk, spot):
        part = part_of(chunk)
        taken = jnp.concatenate(
            [frames[2 * index - 1, part], frames[2 * index, part], frames[2 * index + 1, part]],
            axis=1,
        )
        section[spot] = jnp.dot(taken, tconv[...], preferred_element_type=F32)

    def activation_of(index, chunk, spot, target):
        active[target] = activated(
            section[spot] + bias_row,
            frames[2 * index + 1, part_of(chunk)],
            pick(first, index),
            gain_row,
            pick(limit, index),
            columns,
        )

    def products_of(index, chunk, target):
        products[index, :, part_of(chunk)] = lax.dot_general(
            head[...], active[target], (((1,), (1,)), ((), ())), preferred_element_type=F32
        )

    def tap_block(index, k):
        return products[index, k * taps : (k + 1) * taps]

    arrive(0, 3)
    units = [(index, chunk) for index in (2, 3, 1) for chunk in range(CHUNKS)]
    before_frame_3, before_frame_1 = CHUNKS, 2 * CHUNKS
    for step in range(len(units) + 2):
        if step == 1:
            pl.semaphore_wait(ready_sem.at[0], 5)
            signal(ready_sem.at[1], y_device(2), y_device(-2), z_device(2), z_device(-2))
        if step == before_frame_3:
            arrive(4, 6)
        if step == before_frame_1:
            arrive(11, 13)
        if step == before_frame_1:
            pl.semaphore_wait(ready_sem.at[1], 4)
            signal(ready_sem.at[2], *[y_device(step) for step in range(1, along_y)])
        if step < len(units):
            section_of(*units[step], step % 2)
        if 1 <= step < len(units) + 1:
            activation_of(*units[step - 1], (step - 1) % 2, step % 2)
        if step >= 2:
            products_of(*units[step - 2], (step - 1) % 2)
        if step == before_frame_1 + 1:
            halo_out[0] = spatial_sum(
                tap_block(frame_count - 2, 0) * pick(two, frame_count)
                + tap_block(frame_count - 1, 1) * pick(one, frame_count),
                latent_dim,
                columns,
            )
            halo_out[1] = spatial_sum(
                tap_block(frame_count - 1, 0) * pick(two, frame_count + 1), latent_dim, columns
            )
            halo = pltpu.make_async_remote_copy(
                src_ref=halo_out,
                dst_ref=halo_in,
                send_sem=halo_sem.at[0],
                recv_sem=halo_sem.at[1],
                device_id=after,
                device_id_type=MESH,
            )
            halo.start()

    for chunk in range(CHUNKS):
        part = part_of(chunk)
        section[chunk % 2] = jnp.dot(
            jnp.concatenate([frames[0, part], frames[1, part]], axis=1),
            tconv[channels:, :],
            preferred_element_type=F32,
        )

    latents[1] = spatial_sum(tap_block(1, 2), latent_dim, columns)
    latents[2] = spatial_sum(tap_block(2, 2) + tap_block(1, 1) * pick(one, 2), latent_dim, columns)
    latents[3] = spatial_sum(
        tap_block(3, 2) + tap_block(2, 1) * pick(one, 3) + tap_block(1, 0) * pick(two, 3),
        latent_dim,
        columns,
    )

    arrive(14, 17)
    tokens = dest.shape[1]
    chips = total // CORES
    row = iota((total, 1), 0)
    matches = dest[...] == jnp.where(row < chips, row * CORES + core, (row - chips) * CORES + 1 - core)
    match[...] = jnp.where(matches, 1.0, 0.0).astype(BF16)
    sooner = jnp.where(iota((tokens, tokens), 0) < iota((tokens, tokens), 1), 1.0, 0.0).astype(BF16)
    counts = jnp.dot(match[...], sooner, preferred_element_type=F32)
    rank = jnp.sum(jnp.where(matches, counts, 0.0), axis=0, keepdims=True)
    column = iota((1, total), 1)
    paired = jnp.where(column < chips, column * CORES + core, (column - chips) * CORES + 1 - core)
    pairing[...] = jnp.where(row == paired, 1.0, 0.0).astype(BF16)
    head_bias_column = column_of(head_bias[...])
    mean_column = column_of(mean[...])
    scale_column = column_of(scale[...])

    pl.semaphore_wait(ready_sem.at[2], along_y - 1)
    signal(ready_sem.at[3], x_device(1), x_device(2), x_device(-1))

    for chunk in range(CHUNKS):
        part = part_of(chunk)
        sends[chunk].wait_recv()
        section[chunk % 2] += jnp.dot(
            carried[part, :], tconv[:channels, :], preferred_element_type=F32
        )
        activation_of(0, chunk, chunk % 2, chunk % 2)
        products_of(0, chunk, chunk % 2)

    latents[0] = spatial_sum(tap_block(0, 2), latent_dim, columns)
    latents[1] += spatial_sum(tap_block(0, 1) * pick(one, 1), latent_dim, columns)
    latents[2] += spatial_sum(tap_block(0, 0) * pick(two, 2), latent_dim, columns)
    halo.wait_recv()
    latents[0] += halo_in[0]
    latents[1] += halo_in[1]
    column = lax.rem(iota((1, cells), 1), columns).astype(F32)
    finished = []
    for index in range(frame_count):
        inside = jnp.where(column < pick(limit, index), 1.0, 0.0)
        value = (latents[index] + head_bias_column - mean_column) * scale_column * inside
        finished.append(value.astype(BF16))
    parts = jnp.dot(
        jnp.concatenate(finished, axis=0), unpatch[...], preferred_element_type=F32
    )
    patch_count = cells // 4
    features = jnp.concatenate(
        [
            jnp.concatenate(
                [
                    parts[
                        index * latent_dim : (index + 1) * latent_dim,
                        quarter * patch_count : (quarter + 1) * patch_count,
                    ]
                    for index in range(frame_count)
                ],
                axis=1,
            )
            for quarter in range(4)
        ],
        axis=0,
    )
    ranked = jnp.concatenate(
        [jnp.where(rank == 0.0, features, 0.0), jnp.where(rank == 1.0, features, 0.0)], axis=0
    ).astype(BF16)
    def routed(first_row):
        return lax.dot_general(
            match[first_row : first_row + chips],
            ranked,
            (((1,), (1,)), ((), ())),
            preferred_element_type=F32,
        ).astype(BF16)

    handed[...] = routed(chips)
    swap = pltpu.make_async_remote_copy(
        src_ref=handed,
        dst_ref=taken,
        send_sem=swap_sem.at[0],
        recv_sem=swap_sem.at[1],
        device_id=other_core,
        device_id_type=MESH,
    )
    swap.start()
    kept = jnp.dot(pairing[:, :chips], routed(0), preferred_element_type=F32)
    pl.semaphore_wait(ready_sem.at[3], ALONG_X - 1)
    swap.wait_recv()
    pairs = kept + jnp.dot(pairing[:, chips:], taken[...], preferred_element_type=F32)
    outgoing[...] = pairs.astype(BF16).reshape(outgoing.shape)

    mine = replica * places + place
    home = pltpu.make_async_copy(outgoing.at[mine], out_ref.at[mine], home_sem)
    home.start()

    def hops(offset):
        far_z, far_y, far_x = offset
        return (
            min(far_z, replicas - far_z) + min(far_y, along_y - far_y) + min(far_x, ALONG_X - far_x)
        )

    offsets = [
        (far_z, far_y, far_x)
        for far_z in range(replicas)
        for far_y in range(along_y)
        for far_x in range(ALONG_X)
    ]
    for far_z, far_y, far_x in sorted(offsets, key=hops, reverse=True):
        if not far_z and not far_y and not far_x:
            continue
        to_replica = lax.rem(replica + far_z, replicas)
        to_place = lax.rem(y + far_y, along_y) * ALONG_X + lax.rem(x + far_x, ALONG_X)
        pltpu.make_async_remote_copy(
            src_ref=outgoing.at[to_replica * places + to_place],
            dst_ref=out_ref.at[mine],
            send_sem=send_sem,
            recv_sem=recv_sem,
            device_id=(to_replica, to_place * CORES + core),
            device_id_type=MESH,
        ).start()

    home.wait()
    swap.wait_send()
    for send in sends:
        send.wait_send()
    halo.wait_send()
    others = out_ref.at[pl.ds(0, chips - 1)]
    pltpu.make_async_copy(others, others, recv_sem).wait()
    others = outgoing.at[pl.ds(0, chips - 1)]
    pltpu.make_async_copy(others, others, send_sem).wait()


def on_device(
    replicas,
    shards,
    frames_in,
    clip_frames,
    res_ids,
    token_dest,
    tconv_weight,
    tconv_bias,
    head_gain,
    head_weight,
    head_bias,
    latent_mean,
    latent_scale,
):
    _, frame_count, slots, height, columns, channels = frames_in.shape
    latent_dim = head_weight.shape[-1]
    cells = height * columns
    tokens = token_dest.shape[1]
    clips = clip_frames.shape[1]
    destinations = replicas * shards
    width = 2 * 4 * latent_dim
    places = shards // CORES
    operands = (
        frames_in.reshape(frame_count * slots, cells, channels),
        clip_frames,
        res_ids,
        token_dest.reshape(1, tokens),
        tconv_weight.reshape(3 * channels, channels),
        tconv_bias,
        head_gain,
        jnp.transpose(head_weight, (0, 1, 2, 4, 3)).reshape(27 * latent_dim, channels),
        head_bias.reshape(1, latent_dim),
        latent_mean.reshape(1, latent_dim),
        latent_scale.reshape(1, latent_dim),
    )
    slots_out = pl.pallas_call(
        functools.partial(encode_kernel, replicas, places, height, columns),
        out_shape=pltpu.VMEM((destinations // CORES, CORES, width), BF16),
        in_specs=[pl.BlockSpec(memory_space=pltpu.HBM)] * len(operands),
        out_specs=pl.BlockSpec(memory_space=pltpu.VMEM),
        scratch_shapes=[
            pltpu.VMEM(operand.shape, operand.dtype) for operand in operands
        ]
        + [
            pltpu.VMEM((cells, channels), BF16),
            pltpu.VMEM((2, latent_dim, cells), F32),
            pltpu.VMEM((2, latent_dim, cells), F32),
            pltpu.VMEM((2, cells // CHUNKS, channels), F32),
            pltpu.VMEM((2, cells // CHUNKS, channels), BF16),
            pltpu.VMEM((frame_count, 27 * latent_dim, cells), F32),
            pltpu.VMEM((frame_count, latent_dim, cells), F32),
            pltpu.VMEM((destinations, tokens), BF16),
            pltpu.VMEM((cells, cells), BF16),
            pltpu.VMEM((destinations, destinations), BF16),
            pltpu.VMEM((destinations // CORES, width), BF16),
            pltpu.VMEM((destinations // CORES, width), BF16),
            pltpu.VMEM((destinations // CORES, CORES, width), BF16),
            pltpu.SemaphoreType.DMA((10 + 2 * frame_count,)),
            pltpu.SemaphoreType.DMA((CHUNKS,)),
            pltpu.SemaphoreType.DMA((CHUNKS,)),
            pltpu.SemaphoreType.DMA((2,)),
            pltpu.SemaphoreType.REGULAR((4,)),
            pltpu.SemaphoreType.DMA((2,)),
            pltpu.SemaphoreType.DMA,
            pltpu.SemaphoreType.DMA,
            pltpu.SemaphoreType.DMA,
        ],
        compiler_params=pltpu.CompilerParams(
            collective_id=0, has_side_effects=True, vmem_limit_bytes=60 * 1024 * 1024
        ),
        name="encode_and_route",
    )(*operands)
    return slots_out.reshape(1, 1, destinations, width)


def solution(mesh):
    in_specs = (
        P("dp", "seq", None, None, None, None),
        P("dp", None),
        P("dp", None),
        P("dp", "seq", None),
        P(),
        P(),
        P(),
        P(),
        P(),
        P(),
        P(),
    )
    out_specs = P("dp", "seq", None, None)
    return jax.shard_map(
        functools.partial(on_device, mesh.shape["dp"], mesh.shape["seq"]),
        mesh=mesh,
        in_specs=in_specs,
        out_specs=out_specs,
        check_vma=False,
    )
```

```python
import functools

import jax
import jax.numpy as jnp
from jax import lax
from jax.experimental import pallas as pl
from jax.experimental.pallas import tpu as pltpu
from jax.sharding import PartitionSpec as P

CORES = 2
ALONG_X = 4
CHUNKS = 2
MESH = pl.DeviceIdType.MESH
F32 = jnp.float32
BF16 = jnp.bfloat16


def iota(shape, axis):
    return lax.broadcasted_iota(jnp.int32, shape, axis)


def reorder(rows, source_of):
    source = source_of(iota((rows, 1), 0))
    return jnp.where(iota((rows, rows), 1) == source, 1.0, 0.0).astype(BF16)


def column_of(row):
    count = row.shape[1]
    diagonal = iota((count, count), 0) == iota((count, count), 1)
    return jnp.sum(jnp.where(diagonal, row, 0.0), axis=1, keepdims=True)


def frame_facts(lengths, resolutions, first_frame, total_frames, columns):
    clips = lengths.shape[1]
    earlier = iota((clips, clips), 1) < iota((clips, clips), 0)
    own = iota((clips, clips), 1) == iota((clips, clips), 0)
    starts = jnp.sum(jnp.where(earlier, lengths, 0.0), axis=1, keepdims=True)
    ends = starts + column_of(lengths)
    resolution = jnp.sum(jnp.where(own, resolutions, 0.0), axis=1, keepdims=True)
    frame = (first_frame + iota((clips, 128), 1)).astype(F32)
    belongs = (frame >= starts) & (frame < ends)
    start = jnp.sum(jnp.where(belongs, starts, 0.0), axis=0, keepdims=True)
    kind = jnp.sum(jnp.where(belongs, resolution, 0.0), axis=0, keepdims=True)
    frame = frame[:1]
    exists = frame < float(total_frames)
    first = jnp.where(frame == start, 1.0, 0.0)
    one = jnp.where((frame - 1.0 >= start) & exists, 1.0, 0.0)
    two = jnp.where((frame - 2.0 >= start) & exists, 1.0, 0.0)
    limit = jnp.where(kind == 1.0, float(columns), float(columns * 13 // 20))
    return first, one, two, limit


def pick(row, index):
    return jnp.sum(jnp.where(iota(row.shape, 1) == index, row, 0.0), axis=1, keepdims=True)


def spatial_sum(taps, latent_dim, columns):
    cells = taps.shape[1]
    band = 3 * latent_dim
    cell = iota((1, cells), 1)
    column = lax.rem(cell, columns)
    above = jnp.where(cell >= columns, pltpu.roll(taps[:band], columns, 1), 0.0)
    below = jnp.where(cell < cells - columns, pltpu.roll(taps[2 * band :], cells - columns, 1), 0.0)
    rows = taps[band : 2 * band] + above + below
    left = jnp.where(column >= 1, pltpu.roll(rows[:latent_dim], 1, 1), 0.0)
    right = jnp.where(column < columns - 1, pltpu.roll(rows[2 * latent_dim :], cells - 1, 1), 0.0)
    return rows[latent_dim : 2 * latent_dim] + left + right


def activated(section, passed, first, gain, limit, columns):
    rows, channels = section.shape
    section = jnp.where(first > 0.5, passed.astype(F32), section).astype(BF16).astype(F32)
    mean_square = jnp.sum(section * section, axis=1, keepdims=True) * (1.0 / channels)
    column = lax.rem(iota((rows, 1), 0), columns).astype(F32)
    inside = jnp.where(column < limit, 0.5, 0.0)
    half = section * (lax.rsqrt(mean_square + 1e-06) * 0.5) * gain
    return (half * 2.0 * (inside + inside * jnp.tanh(half))).astype(BF16)


def encode_kernel(
    replicas,
    places,
    height,
    columns,
    frames_hbm,
    clip_hbm,
    res_hbm,
    dest_hbm,
    tconv_hbm,
    bias_hbm,
    gain_hbm,
    head_hbm,
    head_bias_hbm,
    mean_hbm,
    scale_hbm,
    out_ref,
    frames,
    clip,
    res,
    dest,
    tconv,
    bias,
    gain,
    head,
    head_bias,
    mean,
    scale,
    carried,
    halo_in,
    halo_out,
    section,
    active,
    products,
    latents,
    match,
    unpatch,
    dest_other,
    handed,
    taken,
    outgoing,
    load_sem,
    carry_send,
    carry_recv,
    halo_sem,
    ready_sem,
    swap_sem,
    home_sem,
    send_sem,
    recv_sem,
):
    shards = places * CORES
    total = replicas * shards
    along_y = places // ALONG_X
    frame_count = frames.shape[0] // 2
    cells, channels = frames.shape[1:]
    latent_dim = head_bias.shape[1]
    taps = 9 * latent_dim
    replica = lax.axis_index("dp")
    shard = lax.axis_index("seq")
    place = lax.div(shard, CORES)
    core = lax.rem(shard, CORES)
    x = lax.rem(place, ALONG_X)
    y = lax.div(place, ALONG_X)
    after = (replica, lax.rem(shard + 1, shards))
    before = (replica, lax.rem(shard + shards - 1, shards))

    def z_device(step):
        return (lax.rem(replica + step + replicas, replicas), shard)

    def y_device(step):
        return (replica, (lax.rem(y + step + along_y, along_y) * ALONG_X + x) * CORES + core)

    def x_device(step):
        return (replica, (y * ALONG_X + lax.rem(x + step + ALONG_X, ALONG_X)) * CORES + core)

    other_core = (replica, place * CORES + 1 - core)

    barrier = pltpu.get_barrier_semaphore()

    def signal(semaphore, *devices):
        for device in devices:
            pl.semaphore_signal(semaphore, inc=1, device_id=device, device_id_type=MESH)

    wanted = [(tconv_hbm, tconv)]
    wanted += [(frames_hbm.at[pl.ds(3, 3)], frames.at[pl.ds(3, 3)])]
    wanted += [(frames_hbm.at[pl.ds(6, 2)], frames.at[pl.ds(6, 2)]), (head_hbm, head)]
    wanted += [(clip_hbm, clip), (res_hbm, res), (bias_hbm, bias), (gain_hbm, gain)]
    wanted += [(dest_hbm, dest), (head_bias_hbm, head_bias), (mean_hbm, mean), (scale_hbm, scale)]
    wanted += [(frames_hbm.at[pl.ds(0, 3)], frames.at[pl.ds(0, 3)])]
    loads = [
        pltpu.make_async_copy(source, target, load_sem.at[index])
        for index, (source, target) in enumerate(wanted)
    ]
    for load in loads[:2]:
        load.start()
    signal(barrier, before, other_core, x_device(1), x_device(-1))
    signal(barrier, y_device(1), y_device(-1), z_device(1), z_device(-1))
    for load in loads[2:]:
        load.start()

    def arrive(first_load, last_load):
        for load in loads[first_load : last_load + 1]:
            load.wait()

    rows = cells // CHUNKS
    sends = [
        pltpu.make_async_remote_copy(
            src_ref=frames_hbm.at[2 * frame_count - 1, pl.ds(chunk * rows, rows)],
            dst_ref=carried.at[pl.ds(chunk * rows, rows)],
            send_sem=carry_send.at[chunk],
            recv_sem=carry_recv.at[chunk],
            device_id=after,
            device_id_type=MESH,
        )
        for chunk in range(CHUNKS)
    ]
    pl.semaphore_wait(barrier, 8)
    for send in sends:
        send.start()
    signal(ready_sem.at[0], x_device(1), y_device(1), y_device(-1), z_device(1), z_device(-1))

    asked = pltpu.make_async_remote_copy(
        src_ref=dest_hbm,
        dst_ref=dest_other,
        send_sem=swap_sem.at[0],
        recv_sem=swap_sem.at[1],
        device_id=other_core,
        device_id_type=MESH,
    )
    asked.start()

    arrive(4, 7)
    first_frame = shard * frame_count
    first, one, two, limit = frame_facts(
        clip[...].astype(F32), res[...].astype(F32), first_frame, shards * frame_count, columns
    )
    bias_row = bias[...].reshape(1, channels)
    gain_row = gain[...].reshape(1, channels)

    def part_of(chunk):
        return slice(chunk * rows, (chunk + 1) * rows)

    def section_of(index, chunk, spot):
        part = part_of(chunk)
        taken = jnp.concatenate(
            [frames[2 * index - 1, part], frames[2 * index, part], frames[2 * index + 1, part]],
            axis=1,
        )
        section[spot] = jnp.dot(taken, tconv[...], preferred_element_type=F32)

    def activation_of(index, chunk, spot, target):
        active[target] = activated(
            section[spot] + bias_row,
            frames[2 * index + 1, part_of(chunk)],
            pick(first, index),
            gain_row,
            pick(limit, index),
            columns,
        )

    def products_of(index, chunk, target):
        products[index, :, part_of(chunk)] = lax.dot_general(
            head[...], active[target], (((1,), (1,)), ((), ())), preferred_element_type=F32
        )

    def tap_block(index, k):
        return products[index, k * taps : (k + 1) * taps]

    arrive(0, 1)
    units = [(index, chunk) for index in (2, 3, 1) for chunk in range(CHUNKS)]
    before_frame_3, before_frame_1 = CHUNKS, 2 * CHUNKS
    for step in range(len(units) + 2):
        if step == 1:
            pl.semaphore_wait(ready_sem.at[0], 5)
            signal(ready_sem.at[1], y_device(2), y_device(-2), z_device(2), z_device(-2))
        if step == before_frame_3:
            arrive(2, 3)
        if step == before_frame_1:
            arrive(12, 12)
        if step == 5:
            pl.semaphore_wait(ready_sem.at[1], 4)
            signal(ready_sem.at[2], *[y_device(step) for step in range(1, along_y)])
        if step < len(units):
            section_of(*units[step], step % 2)
        if 1 <= step < len(units) + 1:
            activation_of(*units[step - 1], (step - 1) % 2, step % 2)
        if step >= 2:
            products_of(*units[step - 2], (step - 1) % 2)
        if step == before_frame_1 + 1:
            halo_out[0] = spatial_sum(
                tap_block(frame_count - 2, 0) * pick(two, frame_count)
                + tap_block(frame_count - 1, 1) * pick(one, frame_count),
                latent_dim,
                columns,
            )
            halo_out[1] = spatial_sum(
                tap_block(frame_count - 1, 0) * pick(two, frame_count + 1), latent_dim, columns
            )
            halo = pltpu.make_async_remote_copy(
                src_ref=halo_out,
                dst_ref=halo_in,
                send_sem=halo_sem.at[0],
                recv_sem=halo_sem.at[1],
                device_id=after,
                device_id_type=MESH,
            )
            halo.start()

    for chunk in range(CHUNKS):
        part = part_of(chunk)
        section[chunk % 2] = jnp.dot(
            jnp.concatenate([frames[0, part], frames[1, part]], axis=1),
            tconv[channels:, :],
            preferred_element_type=F32,
        )

    latents[1] = spatial_sum(tap_block(1, 2), latent_dim, columns)
    latents[2] = spatial_sum(tap_block(2, 2) + tap_block(1, 1) * pick(one, 2), latent_dim, columns)
    latents[3] = spatial_sum(
        tap_block(3, 2) + tap_block(2, 1) * pick(one, 3) + tap_block(1, 0) * pick(two, 3),
        latent_dim,
        columns,
    )

    def patch_of(cell):
        row, column = lax.div(cell, columns), lax.rem(cell, columns)
        part = lax.rem(row, 2) * 2 + lax.rem(column, 2)
        return part * (cells // 4) + lax.div(row, 2) * (columns // 2) + lax.div(column, 2)

    unpatch[...] = reorder(cells, patch_of)

    tokens = dest.shape[1]
    chips = total // CORES
    row = iota((total, 1), 0)
    source = lax.rem(row, CORES)
    from_here = source == core
    arrive(8, 11)
    asked.wait_recv()
    matches = jnp.where(from_here, dest[...], dest_other[...]) == row - source + core
    match[...] = jnp.where(matches, 1.0, 0.0).astype(BF16)
    token = iota((1, tokens), 1).astype(F32)
    soonest = jnp.min(jnp.where(matches, token, float(tokens)), axis=1, keepdims=True)
    second = jnp.where(matches & (token != soonest), 1.0, 0.0)
    rank = jnp.sum(jnp.where(from_here, second, 0.0), axis=0, keepdims=True)
    rank_other = jnp.sum(jnp.where(from_here, 0.0, second), axis=0, keepdims=True)
    head_bias_column = column_of(head_bias[...])
    mean_column = column_of(mean[...])
    scale_column = column_of(scale[...])


    for chunk in range(CHUNKS):
        part = part_of(chunk)
        sends[chunk].wait_recv()
        section[chunk % 2] += jnp.dot(
            carried[part, :], tconv[:channels, :], preferred_element_type=F32
        )
        activation_of(0, chunk, chunk % 2, chunk % 2)
        products_of(0, chunk, chunk % 2)
        if chunk == 0:
            pl.semaphore_wait(ready_sem.at[2], along_y - 1)
            signal(ready_sem.at[3], x_device(1), x_device(2), x_device(-1))

    latents[0] = spatial_sum(tap_block(0, 2), latent_dim, columns)
    latents[1] += spatial_sum(tap_block(0, 1) * pick(one, 1), latent_dim, columns)
    latents[2] += spatial_sum(tap_block(0, 0) * pick(two, 2), latent_dim, columns)
    halo.wait_recv()
    latents[0] += halo_in[0]
    latents[1] += halo_in[1]
    column = lax.rem(iota((1, cells), 1), columns).astype(F32)
    finished = []
    for index in range(frame_count):
        inside = jnp.where(column < pick(limit, index), 1.0, 0.0)
        value = (latents[index] + head_bias_column - mean_column) * scale_column * inside
        finished.append(value.astype(BF16))
    parts = jnp.dot(
        jnp.concatenate(finished, axis=0), unpatch[...], preferred_element_type=F32
    )
    patch_count = cells // 4
    features = jnp.concatenate(
        [
            jnp.concatenate(
                [
                    parts[
                        index * latent_dim : (index + 1) * latent_dim,
                        quarter * patch_count : (quarter + 1) * patch_count,
                    ]
                    for index in range(frame_count)
                ],
                axis=1,
            )
            for quarter in range(4)
        ],
        axis=0,
    )
    handed[...] = features.astype(BF16)
    swap = pltpu.make_async_remote_copy(
        src_ref=handed,
        dst_ref=taken,
        send_sem=swap_sem.at[2],
        recv_sem=swap_sem.at[3],
        device_id=other_core,
        device_id_type=MESH,
    )
    swap.start()

    def routed(values, ranks):
        ranked = jnp.concatenate(
            [jnp.where(ranks == 0.0, values, 0.0), jnp.where(ranks == 1.0, values, 0.0)], axis=0
        ).astype(BF16)
        return lax.dot_general(
            match[...], ranked, (((1,), (1,)), ((), ())), preferred_element_type=F32
        )

    kept = routed(features, rank)
    pl.semaphore_wait(ready_sem.at[3], ALONG_X - 1)
    swap.wait_recv()
    pairs = jnp.where(from_here, kept, routed(taken[...].astype(F32), rank_other))
    outgoing[...] = pairs.astype(BF16).reshape(outgoing.shape)

    mine = replica * places + place
    home = pltpu.make_async_copy(outgoing.at[mine], out_ref.at[mine], home_sem)
    home.start()

    def hops(offset):
        far_z, far_y, far_x = offset
        return (
            min(far_z, replicas - far_z) + min(far_y, along_y - far_y) + min(far_x, ALONG_X - far_x)
        )

    offsets = [
        (far_z, far_y, far_x)
        for far_z in range(replicas)
        for far_y in range(along_y)
        for far_x in range(ALONG_X)
    ]
    for far_z, far_y, far_x in sorted(offsets, key=hops, reverse=True):
        if not far_z and not far_y and not far_x:
            continue
        to_replica = lax.rem(replica + far_z, replicas)
        to_place = lax.rem(y + far_y, along_y) * ALONG_X + lax.rem(x + far_x, ALONG_X)
        pltpu.make_async_remote_copy(
            src_ref=outgoing.at[to_replica * places + to_place],
            dst_ref=out_ref.at[mine],
            send_sem=send_sem,
            recv_sem=recv_sem,
            device_id=(to_replica, to_place * CORES + core),
            device_id_type=MESH,
        ).start()

    home.wait()
    asked.wait_send()
    swap.wait_send()
    for send in sends:
        send.wait_send()
    halo.wait_send()
    others = out_ref.at[pl.ds(0, chips - 1)]
    pltpu.make_async_copy(others, others, recv_sem).wait()
    others = outgoing.at[pl.ds(0, chips - 1)]
    pltpu.make_async_copy(others, others, send_sem).wait()


def on_device(
    replicas,
    shards,
    frames_in,
    clip_frames,
    res_ids,
    token_dest,
    tconv_weight,
    tconv_bias,
    head_gain,
    head_weight,
    head_bias,
    latent_mean,
    latent_scale,
):
    _, frame_count, slots, height, columns, channels = frames_in.shape
    latent_dim = head_weight.shape[-1]
    cells = height * columns
    tokens = token_dest.shape[1]
    clips = clip_frames.shape[1]
    destinations = replicas * shards
    width = 2 * 4 * latent_dim
    places = shards // CORES
    operands = (
        frames_in.reshape(frame_count * slots, cells, channels),
        clip_frames,
        res_ids,
        token_dest.reshape(1, tokens),
        tconv_weight.reshape(3 * channels, channels),
        tconv_bias,
        head_gain,
        jnp.transpose(head_weight, (0, 1, 2, 4, 3)).reshape(27 * latent_dim, channels),
        head_bias.reshape(1, latent_dim),
        latent_mean.reshape(1, latent_dim),
        latent_scale.reshape(1, latent_dim),
    )
    slots_out = pl.pallas_call(
        functools.partial(encode_kernel, replicas, places, height, columns),
        out_shape=pltpu.VMEM((destinations // CORES, CORES, width), BF16),
        in_specs=[pl.BlockSpec(memory_space=pltpu.HBM)] * len(operands),
        out_specs=pl.BlockSpec(memory_space=pltpu.VMEM),
        scratch_shapes=[
            pltpu.VMEM(operand.shape, operand.dtype) for operand in operands
        ]
        + [
            pltpu.VMEM((cells, channels), BF16),
            pltpu.VMEM((2, latent_dim, cells), F32),
            pltpu.VMEM((2, latent_dim, cells), F32),
            pltpu.VMEM((2, cells // CHUNKS, channels), F32),
            pltpu.VMEM((2, cells // CHUNKS, channels), BF16),
            pltpu.VMEM((frame_count, 27 * latent_dim, cells), F32),
            pltpu.VMEM((frame_count, latent_dim, cells), F32),
            pltpu.VMEM((destinations, tokens), BF16),
            pltpu.VMEM((cells, cells), BF16),
            pltpu.VMEM((1, tokens), jnp.int32),
            pltpu.VMEM((4 * latent_dim, tokens), BF16),
            pltpu.VMEM((4 * latent_dim, tokens), BF16),
            pltpu.VMEM((destinations // CORES, CORES, width), BF16),
            pltpu.SemaphoreType.DMA((13,)),
            pltpu.SemaphoreType.DMA((CHUNKS,)),
            pltpu.SemaphoreType.DMA((CHUNKS,)),
            pltpu.SemaphoreType.DMA((2,)),
            pltpu.SemaphoreType.REGULAR((4,)),
            pltpu.SemaphoreType.DMA((4,)),
            pltpu.SemaphoreType.DMA,
            pltpu.SemaphoreType.DMA,
            pltpu.SemaphoreType.DMA,
        ],
        compiler_params=pltpu.CompilerParams(
            collective_id=0, has_side_effects=True, vmem_limit_bytes=60 * 1024 * 1024
        ),
        name="encode_and_route",
    )(*operands)
    return slots_out.reshape(1, 1, destinations, width)


def solution(mesh):
    in_specs = (
        P("dp", "seq", None, None, None, None),
        P("dp", None),
        P("dp", None),
        P("dp", "seq", None),
        P(),
        P(),
        P(),
        P(),
        P(),
        P(),
        P(),
    )
    out_specs = P("dp", "seq", None, None)
    return jax.shard_map(
        functools.partial(on_device, mesh.shape["dp"], mesh.shape["seq"]),
        mesh=mesh,
        in_specs=in_specs,
        out_specs=out_specs,
        check_vma=False,
    )
```

```python
import functools

import jax
import jax.numpy as jnp
from jax import lax
from jax.experimental import pallas as pl
from jax.experimental.pallas import tpu as pltpu
from jax.sharding import PartitionSpec as P

CORES = 2
ALONG_X = 4
CHUNKS = 2
MESH = pl.DeviceIdType.MESH
F32 = jnp.float32
BF16 = jnp.bfloat16


def iota(shape, axis):
    return lax.broadcasted_iota(jnp.int32, shape, axis)


def reorder(rows, source_of):
    source = source_of(iota((rows, 1), 0))
    return jnp.where(iota((rows, rows), 1) == source, 1.0, 0.0).astype(BF16)


def column_of(row):
    count = row.shape[1]
    diagonal = iota((count, count), 0) == iota((count, count), 1)
    return jnp.sum(jnp.where(diagonal, row, 0.0), axis=1, keepdims=True)


def frame_facts(lengths, resolutions, first_frame, total_frames, columns):
    clips = lengths.shape[1]
    earlier = iota((clips, clips), 1) < iota((clips, clips), 0)
    own = iota((clips, clips), 1) == iota((clips, clips), 0)
    starts = jnp.sum(jnp.where(earlier, lengths, 0.0), axis=1, keepdims=True)
    ends = starts + column_of(lengths)
    resolution = jnp.sum(jnp.where(own, resolutions, 0.0), axis=1, keepdims=True)
    frame = (first_frame + iota((clips, 128), 1)).astype(F32)
    belongs = (frame >= starts) & (frame < ends)
    start = jnp.sum(jnp.where(belongs, starts, 0.0), axis=0, keepdims=True)
    kind = jnp.sum(jnp.where(belongs, resolution, 0.0), axis=0, keepdims=True)
    frame = frame[:1]
    exists = frame < float(total_frames)
    first = jnp.where(frame == start, 1.0, 0.0)
    one = jnp.where((frame - 1.0 >= start) & exists, 1.0, 0.0)
    two = jnp.where((frame - 2.0 >= start) & exists, 1.0, 0.0)
    limit = jnp.where(kind == 1.0, float(columns), float(columns * 13 // 20))
    return first, one, two, limit


def pick(row, index):
    return jnp.sum(jnp.where(iota(row.shape, 1) == index, row, 0.0), axis=1, keepdims=True)


def spatial_sum(taps, latent_dim, columns):
    cells = taps.shape[1]
    band = 3 * latent_dim
    cell = iota((1, cells), 1)
    column = lax.rem(cell, columns)
    above = jnp.where(cell >= columns, pltpu.roll(taps[:band], columns, 1), 0.0)
    below = jnp.where(cell < cells - columns, pltpu.roll(taps[2 * band :], cells - columns, 1), 0.0)
    rows = taps[band : 2 * band] + above + below
    left = jnp.where(column >= 1, pltpu.roll(rows[:latent_dim], 1, 1), 0.0)
    right = jnp.where(column < columns - 1, pltpu.roll(rows[2 * latent_dim :], cells - 1, 1), 0.0)
    return rows[latent_dim : 2 * latent_dim] + left + right


def activated(section, passed, first, gain, limit, columns):
    rows, channels = section.shape
    section = jnp.where(first > 0.5, passed.astype(F32), section).astype(BF16).astype(F32)
    mean_square = jnp.sum(section * section, axis=1, keepdims=True) * (1.0 / channels)
    column = lax.rem(iota((rows, 1), 0), columns).astype(F32)
    inside = jnp.where(column < limit, 0.5, 0.0)
    half = section * (lax.rsqrt(mean_square + 1e-06) * 0.5) * gain
    return (half * 2.0 * (inside + inside * jnp.tanh(half))).astype(BF16)


def encode_kernel(
    replicas,
    places,
    height,
    columns,
    frames_hbm,
    clip_hbm,
    res_hbm,
    dest_hbm,
    tconv_hbm,
    bias_hbm,
    gain_hbm,
    head_hbm,
    head_bias_hbm,
    mean_hbm,
    scale_hbm,
    out_ref,
    frames,
    clip,
    res,
    dest,
    tconv,
    bias,
    gain,
    head,
    head_bias,
    mean,
    scale,
    carried,
    halo_in,
    halo_out,
    section,
    active,
    products,
    latents,
    match,
    unpatch,
    pairing,
    handed,
    taken,
    outgoing,
    load_sem,
    carry_send,
    carry_recv,
    halo_sem,
    ready_sem,
    swap_sem,
    home_sem,
    send_sem,
    recv_sem,
):
    shards = places * CORES
    total = replicas * shards
    along_y = places // ALONG_X
    frame_count = frames.shape[0] // 2
    cells, channels = frames.shape[1:]
    latent_dim = head_bias.shape[1]
    taps = 9 * latent_dim
    replica = lax.axis_index("dp")
    shard = lax.axis_index("seq")
    place = lax.div(shard, CORES)
    core = lax.rem(shard, CORES)
    x = lax.rem(place, ALONG_X)
    y = lax.div(place, ALONG_X)
    after = (replica, lax.rem(shard + 1, shards))
    before = (replica, lax.rem(shard + shards - 1, shards))

    def z_device(step):
        return (lax.rem(replica + step + replicas, replicas), shard)

    def y_device(step):
        return (replica, (lax.rem(y + step + along_y, along_y) * ALONG_X + x) * CORES + core)

    def x_device(step):
        return (replica, (y * ALONG_X + lax.rem(x + step + ALONG_X, ALONG_X)) * CORES + core)

    other_core = (replica, place * CORES + 1 - core)

    barrier = pltpu.get_barrier_semaphore()

    def signal(semaphore, *devices):
        for device in devices:
            pl.semaphore_signal(semaphore, inc=1, device_id=device, device_id_type=MESH)

    signal(barrier, before, other_core, x_device(1), x_device(-1))
    signal(barrier, y_device(1), y_device(-1), z_device(1), z_device(-1))

    wanted = [(tconv_hbm, tconv)]
    wanted += [(frames_hbm.at[index], frames.at[index]) for index in (3, 4, 5, 6, 7)]
    wanted += [(head_hbm, head), (bias_hbm, bias), (gain_hbm, gain), (clip_hbm, clip), (res_hbm, res)]
    wanted += [(frames_hbm.at[index], frames.at[index]) for index in (2, 1, 0)]
    wanted += [(dest_hbm, dest), (head_bias_hbm, head_bias), (mean_hbm, mean), (scale_hbm, scale)]
    loads = [
        pltpu.make_async_copy(source, target, load_sem.at[index])
        for index, (source, target) in enumerate(wanted)
    ]
    for load in loads:
        load.start()

    def arrive(first_load, last_load):
        for load in loads[first_load : last_load + 1]:
            load.wait()

    def patch_of(cell):
        row, column = lax.div(cell, columns), lax.rem(cell, columns)
        part = lax.rem(row, 2) * 2 + lax.rem(column, 2)
        return part * (cells // 4) + lax.div(row, 2) * (columns // 2) + lax.div(column, 2)

    unpatch[...] = reorder(cells, patch_of)


    rows = cells // CHUNKS
    sends = [
        pltpu.make_async_remote_copy(
            src_ref=frames_hbm.at[2 * frame_count - 1, pl.ds(chunk * rows, rows)],
            dst_ref=carried.at[pl.ds(chunk * rows, rows)],
            send_sem=carry_send.at[chunk],
            recv_sem=carry_recv.at[chunk],
            device_id=after,
            device_id_type=MESH,
        )
        for chunk in range(CHUNKS)
    ]
    pl.semaphore_wait(barrier, 8)
    for send in sends:
        send.start()
    signal(ready_sem.at[0], x_device(1), y_device(1), y_device(-1), z_device(1), z_device(-1))

    arrive(7, 10)
    first_frame = shard * frame_count
    first, one, two, limit = frame_facts(
        clip[...].astype(F32), res[...].astype(F32), first_frame, shards * frame_count, columns
    )
    bias_row = bias[...].reshape(1, channels)
    gain_row = gain[...].reshape(1, channels)

    def part_of(chunk):
        return slice(chunk * rows, (chunk + 1) * rows)

    def section_of(index, chunk, spot):
        part = part_of(chunk)
        taken = jnp.concatenate(
            [frames[2 * index - 1, part], frames[2 * index, part], frames[2 * index + 1, part]],
            axis=1,
        )
        section[spot] = jnp.dot(taken, tconv[...], preferred_element_type=F32)

    def activation_of(index, chunk, spot, target):
        active[target] = activated(
            section[spot] + bias_row,
            frames[2 * index + 1, part_of(chunk)],
            pick(first, index),
            gain_row,
            pick(limit, index),
            columns,
        )

    def products_of(index, chunk, target):
        products[index, :, part_of(chunk)] = lax.dot_general(
            head[...], active[target], (((1,), (1,)), ((), ())), preferred_element_type=F32
        )

    def tap_block(index, k):
        return products[index, k * taps : (k + 1) * taps]

    arrive(0, 3)
    units = [(index, chunk) for index in (2, 3, 1) for chunk in range(CHUNKS)]
    before_frame_3, before_frame_1 = CHUNKS, 2 * CHUNKS
    for step in range(len(units) + 2):
        if step == 1:
            pl.semaphore_wait(ready_sem.at[0], 5)
            signal(ready_sem.at[1], y_device(2), y_device(-2), z_device(2), z_device(-2))
        if step == before_frame_3:
            arrive(4, 6)
        if step == before_frame_1:
            arrive(11, 13)
        if step == before_frame_1:
            pl.semaphore_wait(ready_sem.at[1], 4)
            signal(ready_sem.at[2], *[y_device(step) for step in range(1, along_y)])
        if step < len(units):
            section_of(*units[step], step % 2)
        if 1 <= step < len(units) + 1:
            activation_of(*units[step - 1], (step - 1) % 2, step % 2)
        if step >= 2:
            products_of(*units[step - 2], (step - 1) % 2)
        if step == before_frame_1 + 1:
            halo_out[0] = spatial_sum(
                tap_block(frame_count - 2, 0) * pick(two, frame_count)
                + tap_block(frame_count - 1, 1) * pick(one, frame_count),
                latent_dim,
                columns,
            )
            halo_out[1] = spatial_sum(
                tap_block(frame_count - 1, 0) * pick(two, frame_count + 1), latent_dim, columns
            )
            halo = pltpu.make_async_remote_copy(
                src_ref=halo_out,
                dst_ref=halo_in,
                send_sem=halo_sem.at[0],
                recv_sem=halo_sem.at[1],
                device_id=after,
                device_id_type=MESH,
            )
            halo.start()

    for chunk in range(CHUNKS):
        part = part_of(chunk)
        section[chunk % 2] = jnp.dot(
            jnp.concatenate([frames[0, part], frames[1, part]], axis=1),
            tconv[channels:, :],
            preferred_element_type=F32,
        )

    latents[1] = spatial_sum(tap_block(1, 2), latent_dim, columns)
    latents[2] = spatial_sum(tap_block(2, 2) + tap_block(1, 1) * pick(one, 2), latent_dim, columns)
    latents[3] = spatial_sum(
        tap_block(3, 2) + tap_block(2, 1) * pick(one, 3) + tap_block(1, 0) * pick(two, 3),
        latent_dim,
        columns,
    )

    arrive(14, 17)
    tokens = dest.shape[1]
    chips = total // CORES
    row = iota((total, 1), 0)
    matches = dest[...] == jnp.where(row < chips, row * CORES + core, (row - chips) * CORES + 1 - core)
    match[...] = jnp.where(matches, 1.0, 0.0).astype(BF16)
    token = iota((1, tokens), 1).astype(F32)
    soonest = jnp.min(jnp.where(matches, token, float(tokens)), axis=1, keepdims=True)
    rank = jnp.sum(jnp.where(matches & (token != soonest), 1.0, 0.0), axis=0, keepdims=True)
    column = iota((1, total), 1)
    paired = jnp.where(column < chips, column * CORES + core, (column - chips) * CORES + 1 - core)
    pairing[...] = jnp.where(row == paired, 1.0, 0.0).astype(BF16)
    head_bias_column = column_of(head_bias[...])
    mean_column = column_of(mean[...])
    scale_column = column_of(scale[...])

    pl.semaphore_wait(ready_sem.at[2], along_y - 1)
    signal(ready_sem.at[3], x_device(1), x_device(2), x_device(-1))

    for chunk in range(CHUNKS):
        part = part_of(chunk)
        sends[chunk].wait_recv()
        section[chunk % 2] += jnp.dot(
            carried[part, :], tconv[:channels, :], preferred_element_type=F32
        )
        activation_of(0, chunk, chunk % 2, chunk % 2)
        products_of(0, chunk, chunk % 2)

    latents[0] = spatial_sum(tap_block(0, 2), latent_dim, columns)
    latents[1] += spatial_sum(tap_block(0, 1) * pick(one, 1), latent_dim, columns)
    latents[2] += spatial_sum(tap_block(0, 0) * pick(two, 2), latent_dim, columns)
    halo.wait_recv()
    latents[0] += halo_in[0]
    latents[1] += halo_in[1]
    column = lax.rem(iota((1, cells), 1), columns).astype(F32)
    finished = []
    for index in range(frame_count):
        inside = jnp.where(column < pick(limit, index), 1.0, 0.0)
        value = (latents[index] + head_bias_column - mean_column) * scale_column * inside
        finished.append(value.astype(BF16))
    parts = jnp.dot(
        jnp.concatenate(finished, axis=0), unpatch[...], preferred_element_type=F32
    )
    patch_count = cells // 4
    features = jnp.concatenate(
        [
            jnp.concatenate(
                [
                    parts[
                        index * latent_dim : (index + 1) * latent_dim,
                        quarter * patch_count : (quarter + 1) * patch_count,
                    ]
                    for index in range(frame_count)
                ],
                axis=1,
            )
            for quarter in range(4)
        ],
        axis=0,
    )
    ranked = jnp.concatenate(
        [jnp.where(rank == 0.0, features, 0.0), jnp.where(rank == 1.0, features, 0.0)], axis=0
    ).astype(BF16)
    def routed(first_row):
        return lax.dot_general(
            match[first_row : first_row + chips],
            ranked,
            (((1,), (1,)), ((), ())),
            preferred_element_type=F32,
        ).astype(BF16)

    handed[...] = routed(chips)
    swap = pltpu.make_async_remote_copy(
        src_ref=handed,
        dst_ref=taken,
        send_sem=swap_sem.at[0],
        recv_sem=swap_sem.at[1],
        device_id=other_core,
        device_id_type=MESH,
    )
    swap.start()
    kept = jnp.dot(pairing[:, :chips], routed(0), preferred_element_type=F32)
    pl.semaphore_wait(ready_sem.at[3], ALONG_X - 1)
    swap.wait_recv()
    pairs = kept + jnp.dot(pairing[:, chips:], taken[...], preferred_element_type=F32)
    outgoing[...] = pairs.astype(BF16).reshape(outgoing.shape)

    mine = replica * places + place
    home = pltpu.make_async_copy(outgoing.at[mine], out_ref.at[mine], home_sem)
    home.start()

    def hops(offset):
        far_z, far_y, far_x = offset
        return (
            min(far_z, replicas - far_z) + min(far_y, along_y - far_y) + min(far_x, ALONG_X - far_x)
        )

    def spread(offset):
        far_z, far_y, far_x = offset
        return hops(offset), (far_z * 37 + far_y * 23 + far_x * 11) % 64

    offsets = [
        (far_z, far_y, far_x)
        for far_z in range(replicas)
        for far_y in range(along_y)
        for far_x in range(ALONG_X)
    ]
    for far_z, far_y, far_x in sorted(offsets, key=spread, reverse=True):
        if not far_z and not far_y and not far_x:
            continue
        to_replica = lax.rem(replica + far_z, replicas)
        to_place = lax.rem(y + far_y, along_y) * ALONG_X + lax.rem(x + far_x, ALONG_X)
        pltpu.make_async_remote_copy(
            src_ref=outgoing.at[to_replica * places + to_place],
            dst_ref=out_ref.at[mine],
            send_sem=send_sem,
            recv_sem=recv_sem,
            device_id=(to_replica, to_place * CORES + core),
            device_id_type=MESH,
        ).start()

    home.wait()
    swap.wait_send()
    for send in sends:
        send.wait_send()
    halo.wait_send()
    others = out_ref.at[pl.ds(0, chips - 1)]
    pltpu.make_async_copy(others, others, recv_sem).wait()
    others = outgoing.at[pl.ds(0, chips - 1)]
    pltpu.make_async_copy(others, others, send_sem).wait()


def on_device(
    replicas,
    shards,
    frames_in,
    clip_frames,
    res_ids,
    token_dest,
    tconv_weight,
    tconv_bias,
    head_gain,
    head_weight,
    head_bias,
    latent_mean,
    latent_scale,
):
    _, frame_count, slots, height, columns, channels = frames_in.shape
    latent_dim = head_weight.shape[-1]
    cells = height * columns
    tokens = token_dest.shape[1]
    clips = clip_frames.shape[1]
    destinations = replicas * shards
    width = 2 * 4 * latent_dim
    places = shards // CORES
    operands = (
        frames_in.reshape(frame_count * slots, cells, channels),
        clip_frames,
        res_ids,
        token_dest.reshape(1, tokens),
        tconv_weight.reshape(3 * channels, channels),
        tconv_bias,
        head_gain,
        jnp.transpose(head_weight, (0, 1, 2, 4, 3)).reshape(27 * latent_dim, channels),
        head_bias.reshape(1, latent_dim),
        latent_mean.reshape(1, latent_dim),
        latent_scale.reshape(1, latent_dim),
    )
    slots_out = pl.pallas_call(
        functools.partial(encode_kernel, replicas, places, height, columns),
        out_shape=pltpu.VMEM((destinations // CORES, CORES, width), BF16),
        in_specs=[pl.BlockSpec(memory_space=pltpu.HBM)] * len(operands),
        out_specs=pl.BlockSpec(memory_space=pltpu.VMEM),
        scratch_shapes=[
            pltpu.VMEM(operand.shape, operand.dtype) for operand in operands
        ]
        + [
            pltpu.VMEM((cells, channels), BF16),
            pltpu.VMEM((2, latent_dim, cells), F32),
            pltpu.VMEM((2, latent_dim, cells), F32),
            pltpu.VMEM((2, cells // CHUNKS, channels), F32),
            pltpu.VMEM((2, cells // CHUNKS, channels), BF16),
            pltpu.VMEM((frame_count, 27 * latent_dim, cells), F32),
            pltpu.VMEM((frame_count, latent_dim, cells), F32),
            pltpu.VMEM((destinations, tokens), BF16),
            pltpu.VMEM((cells, cells), BF16),
            pltpu.VMEM((destinations, destinations), BF16),
            pltpu.VMEM((destinations // CORES, width), BF16),
            pltpu.VMEM((destinations // CORES, width), BF16),
            pltpu.VMEM((destinations // CORES, CORES, width), BF16),
            pltpu.SemaphoreType.DMA((10 + 2 * frame_count,)),
            pltpu.SemaphoreType.DMA((CHUNKS,)),
            pltpu.SemaphoreType.DMA((CHUNKS,)),
            pltpu.SemaphoreType.DMA((2,)),
            pltpu.SemaphoreType.REGULAR((4,)),
            pltpu.SemaphoreType.DMA((2,)),
            pltpu.SemaphoreType.DMA,
            pltpu.SemaphoreType.DMA,
            pltpu.SemaphoreType.DMA,
        ],
        compiler_params=pltpu.CompilerParams(
            collective_id=0, has_side_effects=True, vmem_limit_bytes=60 * 1024 * 1024
        ),
        name="encode_and_route",
    )(*operands)
    return slots_out.reshape(1, 1, destinations, width)


def solution(mesh):
    in_specs = (
        P("dp", "seq", None, None, None, None),
        P("dp", None),
        P("dp", None),
        P("dp", "seq", None),
        P(),
        P(),
        P(),
        P(),
        P(),
        P(),
        P(),
    )
    out_specs = P("dp", "seq", None, None)
    return jax.shard_map(
        functools.partial(on_device, mesh.shape["dp"], mesh.shape["seq"]),
        mesh=mesh,
        in_specs=in_specs,
        out_specs=out_specs,
        check_vma=False,
    )
```
